256 devices in a mesh: tm: 4 (over y_hi, core), space: 16 (over y_lo, z), head: 4 (over x).
Axes of the slice: x: 4, y: 4 (y_hi: 2, y_lo: 2; y = y_hi * 2 + y_lo), z: 8, core: 2. Of those that a mesh axis runs over, the one named last changes fastest.
Arguments:
- queries: bfloat16 [32, 64, 32, 3072], P('tm', 'space', None, 'head'), may hold values from -6 to 6
- key_rows: bfloat16 [32, 64, 32, 3072], P('tm', 'space', None, 'head'), may hold values from -6 to 6
- value_rows: bfloat16 [32, 64, 32, 3072], P('tm', 'space', None, 'head'), may hold values from -6 to 6
- text_keys: bfloat16 [128, 3072], P('tm', 'head'), may hold values from -6 to 6
- text_values: bfloat16 [128, 3072], P('tm', 'head'), may hold values from -6 to 6
- text_count: int32 [1], replicated, may hold values from 32 to 128
- window_table: int32 [32, 64, 4], replicated, may hold values from 12 to 8191, as said below
Outputs:
- attended: bfloat16 [32, 64, 32, 3072], P('tm', 'space', None, 'head')
The draws below stay inside these ranges and needn't reach their ends.
Inputs may be any that keep to these rules, and one draw needn't show every extreme that they name: `window_table`: each window is a box of whole tiles spanning at most two frames, at most two neighbouring row groups (rows k * 4 to (k + 1) * 4 - 1) and at most two neighbouring tiles; some window spans two in each; tiles of different windows have different ids.
All inputs are finite; a program needn't handle non-finite values.
Results may differ from the reference program's by a relative error of at most 0.0045.
Values may be sent and summed in bfloat16 or wider, within the bound.
A program may use at most 128 MiB of HBM per device.

```python
import math
import jax
import jax.numpy as jnp
from jax import lax

RT = 4
W = 32
TILE = 8
HEADS = 24
HD = 128
TXT = 128
NF = 32
NR = 64


def draw_queries(key, part):
    key = jax.random.fold_in(key, 5)
    shape = (NF, NR, W, HEADS * HD)
    drawn = jnp.clip(jax.random.normal(key, shape, jnp.float32), -6.0, 6.0)
    return drawn.astype(jnp.bfloat16)


def draw_key_rows(key, part):
    key = jax.random.fold_in(key, 7)
    shape = (NF, NR, W, HEADS * HD)
    drawn = jnp.clip(jax.random.normal(key, shape, jnp.float32), -6.0, 6.0)
    return drawn.astype(jnp.bfloat16)


def boundaries(key, count):
    coin_key, place_key = jax.random.split(key)
    coins = jax.random.randint(coin_key, (count,), 0, 2)
    paired = jax.random.randint(place_key, (), 0, count - 1)
    position = jnp.arange(count, dtype=jnp.int32)

    def advance(previous, inputs):
        coin, place = inputs
        opened = jnp.where(place == 0, 1, jnp.where(place == paired, 1, jnp.where(place == paired + 1, 0, jnp.where(previous == 0, 1, coin))))
        opened = opened.astype(jnp.int32)
        return (opened, opened)
    unused, starts = lax.scan(advance, jnp.int32(1), (coins, position))
    groups = (jnp.cumsum(starts) - 1).astype(jnp.int32)
    same_or_before = (groups[None, :] <= groups[:, None]).astype(jnp.int32)
    return (jnp.sum(same_or_before, axis=1) - 1).astype(jnp.int32)


def draw_window_table(key, part):
    key = jax.random.fold_in(key, 9)
    frame_key, row_key, tile_key = jax.random.split(key, 3)
    frame_last = boundaries(frame_key, NF)
    group_last = boundaries(row_key, NR // RT)
    row_last = jnp.repeat(group_last * RT + (RT - 1), RT)
    tile_last = boundaries(tile_key, W // TILE)
    table = (frame_last[:, None, None] * NR + row_last[None, :, None]) * (W // TILE) + tile_last[None, None, :]
    return table.astype(jnp.int32)


def level_of(rng, dims, pieces, low, top_value):
    gain, own = 1.0, jax.random.fold_in(rng, 6)
    for dim, blocks in pieces:
        heights = jnp.exp(jax.random.uniform(jax.random.fold_in(own, dim), (blocks,), jnp.float32, low / len(pieces), top_value / len(pieces)))
        gain = gain * jnp.repeat(heights, dims[dim] // blocks).reshape([-1 if axis == dim else 1 for axis in range(len(dims))])
    return gain


def centred(stream_key, dims, scale, reach, cuts=(), kind=jnp.bfloat16):
    array = jax.random.normal(stream_key, dims, jnp.float32) * scale
    if len(cuts) > 0:
        array = level_of(stream_key, dims, cuts, -0.22, 0.18) * array
    return jnp.clip(array, min=-reach, max=reach).astype(kind)


def setup_inputs(seed: int = 0) -> dict:
    key_of = jax.random.split(jax.random.key(seed), 8)
    queries = draw_queries(jax.random.fold_in(key_of[7], 71), 0)
    key_rows = draw_key_rows(jax.random.fold_in(key_of[7], 71), 0)
    value_rows = centred(key_of[2], (NF, NR, W, HEADS * HD), 1.0, 6.0, ((0, 4), (1, 16), (3, 4)))
    text_keys = centred(key_of[3], (TXT, HEADS * HD), 1.0, 6.0, ((0, 4), (1, 4)))
    text_values = centred(key_of[4], (TXT, HEADS * HD), 1.0, 6.0, ((0, 4), (1, 4)))
    text_count = jax.random.randint(key_of[5], (1,), TXT // 4, TXT + 1).astype(jnp.int32)
    window_table = draw_window_table(jax.random.fold_in(key_of[7], 71), 0)
    return dict(queries=queries, key_rows=key_rows, value_rows=value_rows, text_keys=text_keys, text_values=text_values, text_count=text_count, window_table=window_table)


def reference(queries, key_rows, value_rows, text_keys, text_values, text_count, window_table):
    frame_count, row_count, col_count, feat_count = queries.shape
    head_count = feat_count // HD
    border = ((1, 1), (RT, RT), (0, 0), (0, 0))
    padded_keys = jnp.pad(key_rows, border)
    padded_values = jnp.pad(value_rows, border)
    token_ids = jnp.pad(jnp.repeat(window_table, TILE, axis=2), ((1, 1), (RT, RT), (0, 0)), constant_values=-1)
    text_key32 = text_keys.astype(jnp.float32).reshape(TXT, head_count, HD)
    text_value32 = text_values.astype(jnp.float32).reshape(TXT, head_count, HD)
    text_allowed = jnp.arange(TXT, dtype=jnp.int32) < text_count[0]
    score_scale = 1.0 / math.sqrt(HD)
    zero_index = jnp.int32(0)
    span = 3 * RT

    def one_row(frame_index, row_index):
        group_start = (row_index // RT * RT).astype(jnp.int32)
        query_line = lax.dynamic_slice(queries, (frame_index, row_index, zero_index, zero_index), (1, 1, col_count, feat_count))
        query_line = query_line.reshape(col_count, head_count, HD).astype(jnp.float32)
        near_keys = lax.dynamic_slice(padded_keys, (frame_index, group_start, zero_index, zero_index), (3, span, col_count, feat_count))
        near_keys = near_keys.reshape(3 * span * col_count, head_count, HD).astype(jnp.float32)
        near_values = lax.dynamic_slice(padded_values, (frame_index, group_start, zero_index, zero_index), (3, span, col_count, feat_count))
        near_values = near_values.reshape(3 * span * col_count, head_count, HD).astype(jnp.float32)
        query_ids = lax.dynamic_slice(token_ids, (frame_index + 1, row_index + RT, zero_index), (1, 1, col_count)).reshape(col_count)
        near_ids = lax.dynamic_slice(token_ids, (frame_index, group_start, zero_index), (3, span, col_count)).reshape(3 * span * col_count)
        allowed = jnp.concatenate([query_ids[:, None] == near_ids[None, :], jnp.broadcast_to(text_allowed[None, :], (col_count, TXT))], axis=1)
        key_all = jnp.concatenate([near_keys, text_key32], axis=0)
        value_all = jnp.concatenate([near_values, text_value32], axis=0)
        scores = jnp.einsum('qhd,khd->hqk', query_line, key_all) * score_scale
        scores = jnp.where(allowed[None], scores, -jnp.inf)
        highest = lax.optimization_barrier(jnp.max(scores, axis=2, keepdims=True))
        weights = jnp.exp(scores - highest)
        denominator = lax.optimization_barrier(jnp.sum(weights, axis=2))
        weights_low = lax.optimization_barrier(weights.astype(jnp.bfloat16)).astype(jnp.float32)
        summed = jnp.einsum('hqk,khd->qhd', weights_low, value_all)
        result = summed / jnp.transpose(denominator)[:, :, None]
        return result.reshape(col_count, feat_count).astype(jnp.bfloat16)

    def one_frame(frame_index):
        return lax.map(lambda row_index: one_row(frame_index, row_index), jnp.arange(row_count, dtype=jnp.int32))
    return lax.map(one_frame, jnp.arange(frame_count, dtype=jnp.int32))
```

```python
import functools
import math

import jax
import jax.numpy as jnp
from jax import lax
from jax.experimental import pallas as pl
from jax.experimental.pallas import tpu as pltpu
from jax.sharding import PartitionSpec as P

TILE = 8
HD = 128
MESH = pl.DeviceIdType.MESH
NT = (((1,), (1,)), ((), ()))


def kernel(
    tm_count,
    space_count,
    count_ref,
    table_ref,
    q_ref,
    k_ref,
    v_ref,
    text_k_ref,
    text_v_ref,
    out_ref,
    queries,
    keys,
    values,
    text_keys,
    text_values,
    result,
    ids,
    query_ids,
    weights_ref,
    denominators,
    z_send,
    z_recv,
    t_send,
    t_recv,
    text_send,
    text_recv,
    local_sem,
    out_sem,
):
    frames, rows, cols, feat = q_ref.shape
    heads = feat // HD
    tokens = rows * cols
    text_rows = text_k_ref.shape[0]
    text_total = text_keys.shape[0]
    t = lax.axis_index("tm")
    s = lax.axis_index("space")
    has_low, has_high = s > 0, s < space_count - 1
    has_before, has_after = t > 0, t < tm_count - 1
    low, high = lax.rem(s + space_count - 1, space_count), lax.rem(s + 1, space_count)
    before, after = lax.rem(t + tm_count - 1, tm_count), lax.rem(t + 1, tm_count)
    half = space_count // 2
    crosses_up, crosses_down = s == half - 1, s == half
    relays_up, relays_down = s == space_count - 1, s == 0
    is_middle = jnp.logical_or(crosses_up, crosses_down)
    is_outer = jnp.logical_or(relays_up, relays_down)
    sources = ((k_ref, keys), (v_ref, values))

    def both(*conditions):
        return functools.reduce(jnp.logical_and, conditions)

    def place_of(part):
        if isinstance(part, int) and part < 2:
            frame = 0 if part == 0 else frames - 1
            return (pl.ds(frame, 1),), (pl.ds(frame + 1, 1),)
        lanes = pl.ds(pl.multiple_of((part - 2) * HD, HD), HD)
        inner = (slice(None), slice(None), lanes)
        return (pl.ds(1, frames - 2), *inner), (pl.ds(2, frames - 2), *inner)

    def z_copy(up, which, part, kind=0):
        source, target = sources[which]
        slot = 0 if up else 2
        side = slot // 2
        here, there = place_of(part)
        if kind == 0:
            peer = high if up else low
        elif kind == 1:
            peer = space_count - 1 if up else 0
        else:
            peer = half if up else half - 1
        src = target.at[(2 - slot, *there)] if kind == 2 else source.at[here]
        dst = target.at[(2 - slot if kind == 1 else slot, *there)]
        return pltpu.make_async_remote_copy(
            src_ref=src,
            dst_ref=dst,
            send_sem=z_send.at[side, which, part],
            recv_sem=z_recv.at[1 - side if kind == 1 else side, which, part],
            device_id={"space": peer},
            device_id_type=MESH,
        )

    def t_copy(forward, which, slot):
        source, target = sources[which]
        peer = after if forward else before
        frame = frames - 1 if forward else 0
        place = 0 if forward else frames + 1
        if slot == 1:
            src = source.at[pl.ds(frame, 1)]
        else:
            src = target.at[slot, pl.ds(frame + 1, 1)]
        side = 0 if forward else 1
        return pltpu.make_async_remote_copy(
            src_ref=src,
            dst_ref=target.at[slot, pl.ds(place, 1)],
            send_sem=t_send.at[side, which, slot],
            recv_sem=t_recv.at[side, which, slot],
            device_id={"tm": peer},
            device_id_type=MESH,
        )

    own_rows = pl.ds(pl.multiple_of(t * text_rows, text_rows), text_rows)

    def text_copy(step, which):
        src, target = ((text_k_ref, text_keys), (text_v_ref, text_values))[which]
        return pltpu.make_async_remote_copy(
            src_ref=src,
            dst_ref=target.at[own_rows],
            send_sem=text_send.at[step, which],
            recv_sem=text_recv.at[step, which],
            device_id={"tm": lax.rem(t + step, tm_count)},
            device_id_type=MESH,
        )

    local_copies = [
        pltpu.make_async_copy(q_ref, queries, local_sem.at[0]),
        pltpu.make_async_copy(k_ref, keys.at[1, pl.ds(1, frames)], local_sem.at[1]),
        pltpu.make_async_copy(v_ref, values.at[1, pl.ds(1, frames)], local_sem.at[2]),
        pltpu.make_async_copy(text_k_ref, text_keys.at[own_rows], local_sem.at[3]),
        pltpu.make_async_copy(text_v_ref, text_values.at[own_rows], local_sem.at[4]),
    ]

    barrier = pltpu.get_barrier_semaphore()

    def greet(where):
        pl.semaphore_signal(barrier, inc=1, device_id=where, device_id_type=MESH)

    pl.when(has_low)(lambda: greet({"space": low}))
    pl.when(has_high)(lambda: greet({"space": high}))

    @pl.when(is_middle)
    def _():
        greet({"space": 0})
        greet({"space": space_count - 1})

    @pl.when(is_outer)
    def _():
        greet({"space": half - 1})
        greet({"space": half})

    for step in range(1, tm_count):
        greet({"tm": lax.rem(t + step, tm_count)})
    pl.semaphore_wait(
        barrier,
        has_low.astype(jnp.int32)
        + has_high.astype(jnp.int32)
        + 2 * is_middle.astype(jnp.int32)
        + 2 * is_outer.astype(jnp.int32)
        + (tm_count - 1),
    )

    ways = (
        (True, has_high, crosses_up, relays_up, has_low),
        (False, has_low, crosses_down, relays_down, has_high),
    )

    def relayed(part):
        return part == 1 or part % 2 == 0 and part >= 2

    def start_part(part, through):
        for which in range(2):
            for up, sends, crosses, _, _ in ways:
                if through:
                    straight = both(sends, jnp.logical_not(crosses))
                    pl.when(straight)(z_copy(up, which, part).start)
                    pl.when(crosses)(z_copy(up, which, part, 1).start)
                else:
                    pl.when(sends)(z_copy(up, which, part).start)

    start_part(0, False)
    start_part(1, True)
    for which in range(2):
        pl.when(has_after)(t_copy(True, which, 1).start)
        pl.when(has_before)(t_copy(False, which, 1).start)
    for step in range(1, tm_count):
        for which in range(2):
            text_copy(step, which).start()

    @pl.loop(0, heads // 2)
    def _(pair):
        part = 2 * pair + 2
        start_part(part, True)
        for which in range(2):
            for up, sends, crosses, _, _ in ways:
                now = both(sends, jnp.logical_or(jnp.logical_not(crosses), pair == 0))
                pl.when(now)(z_copy(up, which, part + 1).start)

    for copy in local_copies:
        copy.start()

    blank = jnp.zeros((rows, cols, feat), values.dtype)
    short = jnp.zeros((rows, cols, HD), values.dtype)

    def clear_group(slot):
        for frame in (0, 1, frames + 1):
            values[slot, frame] = blank

        @pl.loop(2, frames)
        def _(frame):
            for head in range(1, heads, 2):
                values[slot, frame, :, :, head * HD : (head + 1) * HD] = short

    def clear_frame(frame):
        for slot in range(3):
            values[slot, frame] = blank

    pl.when(relays_down)(lambda: clear_group(0))
    pl.when(relays_up)(lambda: clear_group(2))
    pl.when(jnp.logical_not(has_before))(lambda: clear_frame(0))
    pl.when(jnp.logical_not(has_after))(lambda: clear_frame(frames + 1))

    tile_count = table_ref.shape[1]
    row_total = table_ref.shape[2]
    frame_total = table_ref.shape[0]
    span = 3 * tokens
    row_at = lax.broadcasted_iota(jnp.int32, (row_total, span), 0)
    lane_at = lax.broadcasted_iota(jnp.int32, (row_total, span), 1)
    row_hit = row_at == s * rows - rows + lane_at // cols
    tile_at = (lane_at // TILE) % tile_count
    high_part = jnp.zeros((frame_total, span), jnp.float32)
    low_part = jnp.zeros((frame_total, span), jnp.float32)
    for tile in range(tile_count):
        pick = jnp.logical_and(row_hit, tile_at == tile).astype(jnp.float32).astype(jnp.bfloat16)
        column = table_ref[:, tile, :]
        for_high = (column // 128).astype(jnp.float32).astype(jnp.bfloat16)
        for_low = (column % 128).astype(jnp.float32).astype(jnp.bfloat16)
        high_part += jnp.dot(for_high, pick, preferred_element_type=jnp.float32)
        low_part += jnp.dot(for_low, pick, preferred_element_type=jnp.float32)
    near_frames = frames + 2
    frame_at = lax.broadcasted_iota(jnp.int32, (2 * frames, frame_total), 1)
    wanted = lax.broadcasted_iota(jnp.int32, (2 * frames, frame_total), 0) + t * frames - 1
    pick = (frame_at == wanted).astype(jnp.float32).astype(jnp.bfloat16)
    near_high = jnp.dot(pick, high_part.astype(jnp.bfloat16), preferred_element_type=jnp.float32)
    near_low = jnp.dot(pick, low_part.astype(jnp.bfloat16), preferred_element_type=jnp.float32)
    near_ids = near_high * 128.0 + near_low
    for frame in range(near_frames):
        ids[frame] = jnp.broadcast_to(near_ids[frame : frame + 1, :], (8, span))

    @pl.loop(0, frames)
    def _(frame):
        row = ids[frame + 1, 0:1, tokens : 2 * tokens]
        query_ids[frame] = jnp.transpose(jnp.broadcast_to(row, (tokens, tokens)))

    def pass_on(part, which):
        for up, _, _, relays, _ in ways:

            @pl.when(relays)
            def _(up=up):
                z_copy(up, which, part, 1).wait_recv()
                z_copy(up, which, part, 2).start()

    for which in range(2):
        pass_on(1, which)
    for part in range(2):
        forward = part == 1
        goes = has_after if forward else has_before
        for which in range(2):
            for up, _, _, _, receives in ways:

                @pl.when(receives)
                def _(up=up, which=which, part=part, forward=forward, goes=goes):
                    z_copy(up, which, part).wait_recv()
                    pl.when(goes)(t_copy(forward, which, 0 if up else 2).start)

    for copy in local_copies:
        copy.wait()

    def wait_halo(which):
        for step in range(1, tm_count):
            text_copy(step, which).wait_recv()
        for slot, there in ((1, None), (0, has_low), (2, has_high)):
            for forward, comes in ((True, has_before), (False, has_after)):
                arrives = comes if there is None else both(comes, there)
                pl.when(arrives)(t_copy(forward, which, slot).wait_recv)

    scale = math.log2(math.e) / math.sqrt(HD)
    text_allowed = lax.broadcasted_iota(jnp.int32, (tokens, text_total), 1) < count_ref[0]

    def out_copy(head):
        lanes = pl.ds(pl.multiple_of(head * HD, HD), HD)
        return pltpu.make_async_copy(
            result.at[:, :, :, lanes], out_ref.at[:, :, :, lanes], out_sem.at[head]
        )

    @pl.loop(0, heads)
    def _(head):
        lanes = pl.ds(pl.multiple_of(head * HD, HD), HD)

        @pl.when(head < heads // 2)
        def _():
            for which in range(2):
                pass_on(2 * head + 2, which)

        @pl.when(head == 0)
        def _():
            wait_halo(0)

        for up, _, _, _, receives in ways:
            pl.when(receives)(z_copy(up, 0, head + 2).wait_recv)

        later = both(lax.rem(head, 2) == 0, head < heads - 2)
        for which in range(2):
            for up, _, crosses, _, _ in ways:
                pl.when(both(crosses, later))(z_copy(up, which, head + 5).start)

        @pl.loop(0, frames)
        def _(frame):
            query = queries[frame, :, :, lanes].reshape(tokens, HD)
            own = query_ids[frame]
            near = pl.ds(frame, 3)
            scores = []
            for slot in range(3):
                key = keys[slot, near, :, :, lanes].reshape(3 * tokens, HD)
                raw = lax.dot_general(query, key, NT, preferred_element_type=jnp.float32)
                for j in range(3):
                    there = ids[frame + j, 0:1, slot * tokens : (slot + 1) * tokens]
                    piece = raw[:, j * tokens : (j + 1) * tokens]
                    scores.append(jnp.where(own == there, piece, -jnp.inf))
            raw = lax.dot_general(
                query, text_keys[:, lanes], NT, preferred_element_type=jnp.float32
            )
            scores.append(jnp.where(text_allowed, raw, -jnp.inf))
            highest = jnp.max(functools.reduce(jnp.maximum, scores), axis=1, keepdims=True)
            weights = [jnp.exp2((score - highest) * scale) for score in scores]
            denominator = jnp.sum(functools.reduce(jnp.add, weights), axis=1, keepdims=True)
            denominators[frame] = jnp.broadcast_to(denominator, (tokens, HD))
            for j, weight in enumerate(weights):
                weights_ref[frame, :, j * tokens : j * tokens + weight.shape[1]] = weight.astype(
                    jnp.bfloat16
                )

        @pl.when(head == 0)
        def _():
            wait_halo(1)

        for up, _, _, _, receives in ways:
            pl.when(receives)(z_copy(up, 1, head + 2).wait_recv)

        @pl.loop(0, frames)
        def _(frame):
            near = pl.ds(frame, 3)
            total = jnp.dot(
                weights_ref[frame, :, 9 * tokens :],
                text_values[:, lanes],
                preferred_element_type=jnp.float32,
            )
            for slot in range(3):
                value = values[slot, near, :, :, lanes].reshape(3 * tokens, HD)
                weight = weights_ref[frame, :, 3 * slot * tokens : 3 * (slot + 1) * tokens]
                total += jnp.dot(weight, value, preferred_element_type=jnp.float32)
            attended = (total / denominators[frame]).astype(jnp.bfloat16)
            result[frame, :, :, lanes] = attended.reshape(rows, cols, HD)

        out_copy(head).start()

    for part in range(heads + 2):
        for which in range(2):
            for up, sends, _, relays, _ in ways:
                out = jnp.logical_or(sends, relays) if relayed(part) else sends
                pl.when(out)(z_copy(up, which, part).wait_send)
    for slot, there in ((1, None), (0, has_low), (2, has_high)):
        for which in range(2):
            for forward, goes in ((True, has_after), (False, has_before)):
                leaves = goes if there is None else both(goes, there)
                pl.when(leaves)(t_copy(forward, which, slot).wait_send)
    for step in range(1, tm_count):
        for which in range(2):
            text_copy(step, which).wait_send()

    @pl.loop(0, heads)
    def _(head):
        out_copy(head).wait()


def per_device(
    tm_count,
    space_count,
    queries,
    key_rows,
    value_rows,
    text_keys,
    text_values,
    text_count,
    window_table,
):
    frames, rows, cols, feat = queries.shape
    heads = feat // HD
    tokens = rows * cols
    text_total = text_keys.shape[0] * tm_count
    table = jnp.transpose(window_table, (0, 2, 1))
    block = (3, frames + 2, rows, cols, feat)
    anywhere = pl.BlockSpec(memory_space=pl.ANY)
    key_total = 9 * tokens + text_total
    flops = 4 * frames * tokens * key_total * feat
    return pl.pallas_call(
        functools.partial(kernel, tm_count, space_count),
        out_shape=jax.ShapeDtypeStruct(queries.shape, queries.dtype),
        in_specs=[
            pl.BlockSpec(memory_space=pltpu.SMEM),
            pl.BlockSpec(memory_space=pltpu.VMEM),
        ]
        + [anywhere] * 5,
        out_specs=anywhere,
        scratch_shapes=[
            pltpu.VMEM(queries.shape, queries.dtype),
            pltpu.VMEM(block, key_rows.dtype),
            pltpu.VMEM(block, value_rows.dtype),
            pltpu.VMEM((text_total, feat), text_keys.dtype),
            pltpu.VMEM((text_total, feat), text_values.dtype),
            pltpu.VMEM(queries.shape, queries.dtype),
            pltpu.VMEM((frames + 2, 8, 3 * tokens), jnp.float32),
            pltpu.VMEM((frames, tokens, tokens), jnp.float32),
            pltpu.VMEM((frames, tokens, key_total), jnp.bfloat16),
            pltpu.VMEM((frames, tokens, HD), jnp.float32),
            pltpu.SemaphoreType.DMA((2, 2, heads + 2)),
            pltpu.SemaphoreType.DMA((2, 2, heads + 2)),
            pltpu.SemaphoreType.DMA((2, 2, 3)),
            pltpu.SemaphoreType.DMA((2, 2, 3)),
            pltpu.SemaphoreType.DMA((tm_count, 2)),
            pltpu.SemaphoreType.DMA((tm_count, 2)),
            pltpu.SemaphoreType.DMA((5,)),
            pltpu.SemaphoreType.DMA((heads,)),
        ],
        compiler_params=pltpu.CompilerParams(
            collective_id=0, has_side_effects=True, vmem_limit_bytes=56 * 2**20
        ),
        cost_estimate=pl.CostEstimate(
            flops=flops, bytes_accessed=4 * queries.size * 2, transcendentals=0
        ),
    )(text_count, table, queries, key_rows, value_rows, text_keys, text_values)


def solution(mesh):
    in_specs = (
        P("tm", "space", None, "head"),
        P("tm", "space", None, "head"),
        P("tm", "space", None, "head"),
        P("tm", "head"),
        P("tm", "head"),
        P(),
        P(),
    )
    out_specs = P("tm", "space", None, "head")
    return jax.shard_map(
        functools.partial(per_device, mesh.shape["tm"], mesh.shape["space"]),
        mesh=mesh,
        in_specs=in_specs,
        out_specs=out_specs,
        check_vma=False,
    )
```

```python
import functools
import math

import jax
import jax.numpy as jnp
from jax import lax
from jax.experimental import pallas as pl
from jax.experimental.pallas import tpu as pltpu
from jax.sharding import PartitionSpec as P

TILE = 8
HD = 128
MESH = pl.DeviceIdType.MESH
NT = (((1,), (1,)), ((), ()))


def kernel(
    tm_count,
    space_count,
    count_ref,
    table_ref,
    q_ref,
    k_ref,
    v_ref,
    text_k_ref,
    text_v_ref,
    out_ref,
    queries,
    keys,
    values,
    text_keys,
    text_values,
    count,
    table,
    ids,
    query_ids,
    weights_ref,
    denominators,
    z_send,
    z_recv,
    t_send,
    t_recv,
    text_send,
    text_recv,
    local_sem,
):
    frames, rows, cols, feat = q_ref.shape
    heads = feat // HD
    tokens = rows * cols
    text_rows = text_k_ref.shape[0]
    text_total = text_keys.shape[0]
    t = lax.axis_index("tm")
    s = lax.axis_index("space")
    has_low, has_high = s > 0, s < space_count - 1
    has_before, has_after = t > 0, t < tm_count - 1
    low, high = lax.rem(s + space_count - 1, space_count), lax.rem(s + 1, space_count)
    before, after = lax.rem(t + tm_count - 1, tm_count), lax.rem(t + 1, tm_count)
    half = space_count // 2
    crosses_up, crosses_down = s == half - 1, s == half
    relays_up, relays_down = s == space_count - 1, s == 0
    is_middle = jnp.logical_or(crosses_up, crosses_down)
    is_outer = jnp.logical_or(relays_up, relays_down)
    sources = ((k_ref, keys), (v_ref, values))

    def both(*conditions):
        return functools.reduce(jnp.logical_and, conditions)

    def place_of(part):
        if isinstance(part, int) and part < 2:
            frame = 0 if part == 0 else frames - 1
            return (pl.ds(frame, 1),), (pl.ds(frame + 1, 1),)
        lanes = pl.ds(pl.multiple_of((part - 2) * HD, HD), HD)
        inner = (slice(None), slice(None), lanes)
        return (pl.ds(1, frames - 2), *inner), (pl.ds(2, frames - 2), *inner)

    def z_copy(up, which, part, kind=0):
        source, target = sources[which]
        slot = 0 if up else 2
        side = slot // 2
        here, there = place_of(part)
        if kind == 0:
            peer = high if up else low
        elif kind == 1:
            peer = space_count - 1 if up else 0
        else:
            peer = half if up else half - 1
        src = target.at[(2 - slot, *there)] if kind == 2 else source.at[here]
        dst = target.at[(2 - slot if kind == 1 else slot, *there)]
        return pltpu.make_async_remote_copy(
            src_ref=src,
            dst_ref=dst,
            send_sem=z_send.at[side, which, part],
            recv_sem=z_recv.at[1 - side if kind == 1 else side, which, part],
            device_id={"space": peer},
            device_id_type=MESH,
        )

    def t_copy(forward, which, slot):
        source, target = sources[which]
        peer = after if forward else before
        frame = frames - 1 if forward else 0
        place = 0 if forward else frames + 1
        if slot == 1:
            src = source.at[pl.ds(frame, 1)]
        else:
            src = target.at[slot, pl.ds(frame + 1, 1)]
        side = 0 if forward else 1
        return pltpu.make_async_remote_copy(
            src_ref=src,
            dst_ref=target.at[slot, pl.ds(place, 1)],
            send_sem=t_send.at[side, which, slot],
            recv_sem=t_recv.at[side, which, slot],
            device_id={"tm": peer},
            device_id_type=MESH,
        )

    own_rows = pl.ds(pl.multiple_of(t * text_rows, text_rows), text_rows)

    def text_copy(step, which):
        src, target = ((text_k_ref, text_keys), (text_v_ref, text_values))[which]
        return pltpu.make_async_remote_copy(
            src_ref=src,
            dst_ref=target.at[own_rows],
            send_sem=text_send.at[step, which],
            recv_sem=text_recv.at[step, which],
            device_id={"tm": lax.rem(t + step, tm_count)},
            device_id_type=MESH,
        )

    first_copies = [
        pltpu.make_async_copy(count_ref, count, local_sem.at[5]),
        pltpu.make_async_copy(table_ref, table, local_sem.at[6]),
    ]
    local_copies = [
        pltpu.make_async_copy(q_ref, queries, local_sem.at[0]),
        pltpu.make_async_copy(k_ref, keys.at[1, pl.ds(1, frames)], local_sem.at[1]),
        pltpu.make_async_copy(v_ref, values.at[1, pl.ds(1, frames)], local_sem.at[2]),
        pltpu.make_async_copy(text_k_ref, text_keys.at[own_rows], local_sem.at[3]),
        pltpu.make_async_copy(text_v_ref, text_values.at[own_rows], local_sem.at[4]),
    ]

    barrier = pltpu.get_barrier_semaphore()

    for copy in first_copies:
        copy.start()

    def greet(where):
        pl.semaphore_signal(barrier, inc=1, device_id=where, device_id_type=MESH)

    pl.when(has_low)(lambda: greet({"space": low}))
    pl.when(has_high)(lambda: greet({"space": high}))

    @pl.when(is_middle)
    def _():
        greet({"space": 0})
        greet({"space": space_count - 1})

    @pl.when(is_outer)
    def _():
        greet({"space": half - 1})
        greet({"space": half})

    for step in range(1, tm_count):
        greet({"tm": lax.rem(t + step, tm_count)})
    pl.semaphore_wait(
        barrier,
        has_low.astype(jnp.int32)
        + has_high.astype(jnp.int32)
        + 2 * is_middle.astype(jnp.int32)
        + 2 * is_outer.astype(jnp.int32)
        + (tm_count - 1),
    )

    ways = (
        (True, has_high, crosses_up, relays_up, has_low),
        (False, has_low, crosses_down, relays_down, has_high),
    )

    def relayed(part):
        return part == 1 or part % 2 == 0 and part >= 2

    def start_part(part, through):
        for which in range(2):
            for up, sends, crosses, _, _ in ways:
                if through:
                    straight = both(sends, jnp.logical_not(crosses))
                    pl.when(straight)(z_copy(up, which, part).start)
                    pl.when(crosses)(z_copy(up, which, part, 1).start)
                else:
                    pl.when(sends)(z_copy(up, which, part).start)

    start_part(0, False)
    start_part(1, True)
    for which in range(2):
        pl.when(has_after)(t_copy(True, which, 1).start)
        pl.when(has_before)(t_copy(False, which, 1).start)
    for step in range(1, tm_count):
        for which in range(2):
            text_copy(step, which).start()

    @pl.loop(0, heads // 2)
    def _(pair):
        part = 2 * pair + 2
        start_part(part, True)
        for which in range(2):
            for up, sends, crosses, _, _ in ways:
                now = both(sends, jnp.logical_or(jnp.logical_not(crosses), pair == 0))
                pl.when(now)(z_copy(up, which, part + 1).start)

    for copy in local_copies:
        copy.start()

    blank = jnp.zeros((rows, cols, feat), values.dtype)
    short = jnp.zeros((rows, cols, HD), values.dtype)

    def clear_group(slot):
        for frame in (0, 1, frames + 1):
            values[slot, frame] = blank

        @pl.loop(2, frames)
        def _(frame):
            for head in range(1, heads, 2):
                values[slot, frame, :, :, head * HD : (head + 1) * HD] = short

    def clear_frame(frame):
        for slot in range(3):
            values[slot, frame] = blank

    pl.when(relays_down)(lambda: clear_group(0))
    pl.when(relays_up)(lambda: clear_group(2))
    pl.when(jnp.logical_not(has_before))(lambda: clear_frame(0))
    pl.when(jnp.logical_not(has_after))(lambda: clear_frame(frames + 1))

    for copy in first_copies:
        copy.wait()
    frame_total, tile_count, row_total = table.shape
    span = 3 * tokens
    row_at = lax.broadcasted_iota(jnp.int32, (row_total, span), 0)
    lane_at = lax.broadcasted_iota(jnp.int32, (row_total, span), 1)
    row_hit = row_at == s * rows - rows + lane_at // cols
    tile_at = (lane_at // TILE) % tile_count
    high_part = jnp.zeros((frame_total, span), jnp.float32)
    low_part = jnp.zeros((frame_total, span), jnp.float32)
    for tile in range(tile_count):
        pick = jnp.logical_and(row_hit, tile_at == tile).astype(jnp.float32).astype(jnp.bfloat16)
        column = table[:, tile, :]
        for_high = (column // 128).astype(jnp.float32).astype(jnp.bfloat16)
        for_low = (column % 128).astype(jnp.float32).astype(jnp.bfloat16)
        high_part += jnp.dot(for_high, pick, preferred_element_type=jnp.float32)
        low_part += jnp.dot(for_low, pick, preferred_element_type=jnp.float32)
    near_frames = frames + 2
    frame_at = lax.broadcasted_iota(jnp.int32, (2 * frames, frame_total), 1)
    wanted = lax.broadcasted_iota(jnp.int32, (2 * frames, frame_total), 0) + t * frames - 1
    pick = (frame_at == wanted).astype(jnp.float32).astype(jnp.bfloat16)
    near_high = jnp.dot(pick, high_part.astype(jnp.bfloat16), preferred_element_type=jnp.float32)
    near_low = jnp.dot(pick, low_part.astype(jnp.bfloat16), preferred_element_type=jnp.float32)
    near_ids = near_high * 128.0 + near_low
    for frame in range(near_frames):
        ids[frame] = jnp.broadcast_to(near_ids[frame : frame + 1, :], (8, span))

    @pl.loop(0, frames)
    def _(frame):
        row = ids[frame + 1, 0:1, tokens : 2 * tokens]
        query_ids[frame] = jnp.transpose(jnp.broadcast_to(row, (tokens, tokens)))

    def pass_on(part, which):
        for up, _, _, relays, _ in ways:

            @pl.when(relays)
            def _(up=up):
                z_copy(up, which, part, 1).wait_recv()
                z_copy(up, which, part, 2).start()

    for which in range(2):
        pass_on(1, which)
    for part in range(2):
        forward = part == 1
        goes = has_after if forward else has_before
        for which in range(2):
            for up, _, _, _, receives in ways:

                @pl.when(receives)
                def _(up=up, which=which, part=part, forward=forward, goes=goes):
                    z_copy(up, which, part).wait_recv()
                    pl.when(goes)(t_copy(forward, which, 0 if up else 2).start)

    for copy in local_copies:
        copy.wait()

    def wait_halo(which):
        for step in range(1, tm_count):
            text_copy(step, which).wait_recv()
        for slot, there in ((1, None), (0, has_low), (2, has_high)):
            for forward, comes in ((True, has_before), (False, has_after)):
                arrives = comes if there is None else both(comes, there)
                pl.when(arrives)(t_copy(forward, which, slot).wait_recv)

    scale = math.log2(math.e) / math.sqrt(HD)
    text_allowed = lax.broadcasted_iota(jnp.int32, (tokens, text_total), 1) < count[0]

    @pl.loop(0, heads)
    def _(head):
        lanes = pl.ds(pl.multiple_of(head * HD, HD), HD)

        @pl.when(head < heads // 2)
        def _():
            for which in range(2):
                pass_on(2 * head + 2, which)

        @pl.when(head == 0)
        def _():
            wait_halo(0)

        for up, _, _, _, receives in ways:
            pl.when(receives)(z_copy(up, 0, head + 2).wait_recv)

        later = both(lax.rem(head, 2) == 0, head < heads - 2)
        for which in range(2):
            for up, _, crosses, _, _ in ways:
                pl.when(both(crosses, later))(z_copy(up, which, head + 5).start)

        @pl.loop(0, frames, unroll=True)
        def _(frame):
            query = queries[frame, :, :, lanes].reshape(tokens, HD)
            own = query_ids[frame]
            near = pl.ds(frame, 3)
            scores = []
            for slot in range(3):
                key = keys[slot, near, :, :, lanes].reshape(3 * tokens, HD)
                raw = lax.dot_general(query, key, NT, preferred_element_type=jnp.float32)
                for j in range(3):
                    there = ids[frame + j, 0:1, slot * tokens : (slot + 1) * tokens]
                    piece = raw[:, j * tokens : (j + 1) * tokens]
                    scores.append(jnp.where(own == there, piece, -jnp.inf))
            raw = lax.dot_general(
                query, text_keys[:, lanes], NT, preferred_element_type=jnp.float32
            )
            scores.append(jnp.where(text_allowed, raw, -jnp.inf))
            highest = jnp.max(functools.reduce(jnp.maximum, scores), axis=1, keepdims=True)
            weights = [jnp.exp2((score - highest) * scale) for score in scores]
            denominator = jnp.sum(functools.reduce(jnp.add, weights), axis=1, keepdims=True)
            denominators[frame] = jnp.broadcast_to(denominator, (tokens, HD))
            for j, weight in enumerate(weights):
                weights_ref[frame, :, j * tokens : j * tokens + weight.shape[1]] = weight.astype(
                    jnp.bfloat16
                )

        @pl.when(head == 0)
        def _():
            wait_halo(1)

        for up, _, _, _, receives in ways:
            pl.when(receives)(z_copy(up, 1, head + 2).wait_recv)

        @pl.loop(0, frames, unroll=True)
        def _(frame):
            near = pl.ds(frame, 3)
            total = jnp.dot(
                weights_ref[frame, :, 9 * tokens :],
                text_values[:, lanes],
                preferred_element_type=jnp.float32,
            )
            for slot in range(3):
                value = values[slot, near, :, :, lanes].reshape(3 * tokens, HD)
                weight = weights_ref[frame, :, 3 * slot * tokens : 3 * (slot + 1) * tokens]
                total += jnp.dot(weight, value, preferred_element_type=jnp.float32)
            attended = (total / denominators[frame]).astype(jnp.bfloat16)
            out_ref[frame, :, :, lanes] = attended.reshape(rows, cols, HD)

    for part in range(heads + 2):
        for which in range(2):
            for up, sends, _, relays, _ in ways:
                out = jnp.logical_or(sends, relays) if relayed(part) else sends
                pl.when(out)(z_copy(up, which, part).wait_send)
    for slot, there in ((1, None), (0, has_low), (2, has_high)):
        for which in range(2):
            for forward, goes in ((True, has_after), (False, has_before)):
                leaves = goes if there is None else both(goes, there)
                pl.when(leaves)(t_copy(forward, which, slot).wait_send)
    for step in range(1, tm_count):
        for which in range(2):
            text_copy(step, which).wait_send()


def per_device(
    tm_count,
    space_count,
    queries,
    key_rows,
    value_rows,
    text_keys,
    text_values,
    text_count,
    window_table,
):
    frames, rows, cols, feat = queries.shape
    heads = feat // HD
    tokens = rows * cols
    text_total = text_keys.shape[0] * tm_count
    table = jnp.transpose(window_table, (0, 2, 1))
    block = (3, frames + 2, rows, cols, feat)
    anywhere = pl.BlockSpec(memory_space=pl.ANY)
    key_total = 9 * tokens + text_total
    flops = 4 * frames * tokens * key_total * feat
    return pl.pallas_call(
        functools.partial(kernel, tm_count, space_count),
        out_shape=pltpu.VMEM(queries.shape, queries.dtype),
        in_specs=[anywhere] * 7,
        out_specs=pl.BlockSpec(memory_space=pltpu.VMEM),
        scratch_shapes=[
            pltpu.VMEM(queries.shape, queries.dtype),
            pltpu.VMEM(block, key_rows.dtype),
            pltpu.VMEM(block, value_rows.dtype),
            pltpu.VMEM((text_total, feat), text_keys.dtype),
            pltpu.VMEM((text_total, feat), text_values.dtype),
            pltpu.SMEM(text_count.shape, text_count.dtype),
            pltpu.VMEM(table.shape, table.dtype),
            pltpu.VMEM((frames + 2, 8, 3 * tokens), jnp.float32),
            pltpu.VMEM((frames, tokens, tokens), jnp.float32),
            pltpu.VMEM((frames, tokens, key_total), jnp.bfloat16),
            pltpu.VMEM((frames, tokens, HD), jnp.float32),
            pltpu.SemaphoreType.DMA((2, 2, heads + 2)),
            pltpu.SemaphoreType.DMA((2, 2, heads + 2)),
            pltpu.SemaphoreType.DMA((2, 2, 3)),
            pltpu.SemaphoreType.DMA((2, 2, 3)),
            pltpu.SemaphoreType.DMA((tm_count, 2)),
            pltpu.SemaphoreType.DMA((tm_count, 2)),
            pltpu.SemaphoreType.DMA((7,)),
        ],
        compiler_params=pltpu.CompilerParams(
            collective_id=0, has_side_effects=True, vmem_limit_bytes=56 * 2**20
        ),
        cost_estimate=pl.CostEstimate(
            flops=flops, bytes_accessed=4 * queries.size * 2, transcendentals=0
        ),
    )(text_count, table, queries, key_rows, value_rows, text_keys, text_values)


def solution(mesh):
    in_specs = (
        P("tm", "space", None, "head"),
        P("tm", "space", None, "head"),
        P("tm", "space", None, "head"),
        P("tm", "head"),
        P("tm", "head"),
        P(),
        P(),
    )
    out_specs = P("tm", "space", None, "head")
    return jax.shard_map(
        functools.partial(per_device, mesh.shape["tm"], mesh.shape["space"]),
        mesh=mesh,
        in_specs=in_specs,
        out_specs=out_specs,
        check_vma=False,
    )
```

```python
import functools
import math

import jax
import jax.numpy as jnp
from jax import lax
from jax.experimental import pallas as pl
from jax.experimental.pallas import tpu as pltpu
from jax.sharding import PartitionSpec as P

TILE = 8
HD = 128
MESH = pl.DeviceIdType.MESH
NT = (((1,), (1,)), ((), ()))


def kernel(
    tm_count,
    space_count,
    count_ref,
    table_ref,
    q_ref,
    k_ref,
    v_ref,
    text_k_ref,
    text_v_ref,
    out_ref,
    queries,
    keys,
    values,
    text_keys,
    text_values,
    count,
    table,
    ids,
    query_ids,
    weights_ref,
    denominators,
    z_send,
    z_recv,
    t_send,
    t_recv,
    text_send,
    text_recv,
    local_sem,
):
    frames, rows, cols, feat = q_ref.shape
    heads = feat // HD
    tokens = rows * cols
    text_rows = text_k_ref.shape[0]
    text_total = text_keys.shape[0]
    t = lax.axis_index("tm")
    s = lax.axis_index("space")
    has_low, has_high = s > 0, s < space_count - 1
    has_before, has_after = t > 0, t < tm_count - 1
    low, high = lax.rem(s + space_count - 1, space_count), lax.rem(s + 1, space_count)
    before, after = lax.rem(t + tm_count - 1, tm_count), lax.rem(t + 1, tm_count)
    half = space_count // 2
    crosses_up, crosses_down = s == half - 1, s == half
    relays_up, relays_down = s == space_count - 1, s == 0
    is_middle = jnp.logical_or(crosses_up, crosses_down)
    is_outer = jnp.logical_or(relays_up, relays_down)
    sources = ((k_ref, keys), (v_ref, values))

    def both(*conditions):
        return functools.reduce(jnp.logical_and, conditions)

    last, rest = heads + 1, heads + 2

    def place_of(which, part):
        if isinstance(part, int) and part < 2:
            frame = 0 if part == 0 else frames - 1
            return (pl.ds(frame, 1),), (pl.ds(frame + 1, 1),)
        start, size, head = 1, frames - 2, part - 2
        if isinstance(part, int) and which == 1:
            if part == last:
                size = frames - 3
            elif part == rest:
                start, size, head = frames - 2, 1, heads - 1
        lanes = pl.ds(pl.multiple_of(head * HD, HD), HD)
        inner = (slice(None), slice(None), lanes)
        return (pl.ds(start, size), *inner), (pl.ds(start + 1, size), *inner)

    def z_copy(up, which, part, kind=0):
        source, target = sources[which]
        slot = 0 if up else 2
        side = slot // 2
        here, there = place_of(which, part)
        if kind == 0:
            peer = high if up else low
        elif kind == 1:
            peer = space_count - 1 if up else 0
        else:
            peer = half if up else half - 1
        src = target.at[(2 - slot, *there)] if kind == 2 else source.at[here]
        dst = target.at[(2 - slot if kind == 1 else slot, *there)]
        return pltpu.make_async_remote_copy(
            src_ref=src,
            dst_ref=dst,
            send_sem=z_send.at[side, which, part],
            recv_sem=z_recv.at[1 - side if kind == 1 else side, which, part],
            device_id={"space": peer},
            device_id_type=MESH,
        )

    def t_copy(forward, which, slot):
        source, target = sources[which]
        peer = after if forward else before
        frame = frames - 1 if forward else 0
        place = 0 if forward else frames + 1
        if slot == 1:
            src = source.at[pl.ds(frame, 1)]
        else:
            src = target.at[slot, pl.ds(frame + 1, 1)]
        side = 0 if forward else 1
        return pltpu.make_async_remote_copy(
            src_ref=src,
            dst_ref=target.at[slot, pl.ds(place, 1)],
            send_sem=t_send.at[side, which, slot],
            recv_sem=t_recv.at[side, which, slot],
            device_id={"tm": peer},
            device_id_type=MESH,
        )

    def passes_corner(forward, slot):
        goes = has_after if forward else has_before
        return goes if slot == 1 else both(goes, has_low if slot == 0 else has_high)

    own_rows = pl.ds(pl.multiple_of(t * text_rows, text_rows), text_rows)

    def text_copy(forward, which, hop):
        src, target = ((text_k_ref, text_keys), (text_v_ref, text_values))[which]
        slab = lax.rem(t + (tm_count - hop if forward else hop), tm_count)
        place = pl.ds(pl.multiple_of(slab * text_rows, text_rows), text_rows)
        side = 0 if forward else 1
        return pltpu.make_async_remote_copy(
            src_ref=src if hop == 0 else target.at[place],
            dst_ref=target.at[place],
            send_sem=text_send.at[side, which, hop],
            recv_sem=text_recv.at[side, which, hop],
            device_id={"tm": after if forward else before},
            device_id_type=MESH,
        )

    def text_ways(hop):
        return (
            (True, t >= hop, both(t >= hop, has_after)),
            (False, t < tm_count - hop, both(t < tm_count - hop, has_before)),
        )

    def text_hop(which, hop):
        for forward, comes, goes in text_ways(hop):
            if hop > 0:
                pl.when(comes)(text_copy(forward, which, hop - 1).wait_recv)
            if hop < tm_count - 1:
                pl.when(goes)(text_copy(forward, which, hop).start)

    first_copies = [
        pltpu.make_async_copy(count_ref, count, local_sem.at[5]),
        pltpu.make_async_copy(table_ref, table, local_sem.at[6]),
    ]
    local_copies = [
        pltpu.make_async_copy(q_ref, queries, local_sem.at[0]),
        pltpu.make_async_copy(k_ref, keys.at[1, pl.ds(1, frames)], local_sem.at[1]),
        pltpu.make_async_copy(v_ref, values.at[1, pl.ds(1, frames)], local_sem.at[2]),
        pltpu.make_async_copy(text_k_ref, text_keys.at[own_rows], local_sem.at[3]),
        pltpu.make_async_copy(text_v_ref, text_values.at[own_rows], local_sem.at[4]),
    ]

    barrier = pltpu.get_barrier_semaphore()

    for copy in first_copies:
        copy.start()

    def greet(where):
        pl.semaphore_signal(barrier, inc=1, device_id=where, device_id_type=MESH)

    pl.when(has_low)(lambda: greet({"space": low}))
    pl.when(has_high)(lambda: greet({"space": high}))

    @pl.when(is_middle)
    def _():
        greet({"space": 0})
        greet({"space": space_count - 1})

    @pl.when(is_outer)
    def _():
        greet({"space": half - 1})
        greet({"space": half})

    pl.when(has_before)(lambda: greet({"tm": before}))
    pl.when(has_after)(lambda: greet({"tm": after}))
    pl.semaphore_wait(
        barrier,
        has_low.astype(jnp.int32)
        + has_high.astype(jnp.int32)
        + 2 * is_middle.astype(jnp.int32)
        + 2 * is_outer.astype(jnp.int32)
        + has_before.astype(jnp.int32)
        + has_after.astype(jnp.int32),
    )

    ways = (
        (True, has_high, crosses_up, relays_up, has_low),
        (False, has_low, crosses_down, relays_down, has_high),
    )

    def relayed(part):
        return part % 2 == 0 and part >= 2

    def start_part(part, through):
        for which in range(2):
            for up, sends, crosses, _, _ in ways:
                if through:
                    straight = both(sends, jnp.logical_not(crosses))
                    pl.when(straight)(z_copy(up, which, part).start)
                    pl.when(crosses)(z_copy(up, which, part, 1).start)
                else:
                    pl.when(sends)(z_copy(up, which, part).start)

    for which in range(2):
        text_hop(which, 0)
    start_part(0, False)
    start_part(1, False)
    for which in range(2):
        pl.when(has_after)(t_copy(True, which, 1).start)
        pl.when(has_before)(t_copy(False, which, 1).start)

    for part in range(2, heads + 2, 2):
        start_part(part, True)
        for which in range(2):
            for up, sends, crosses, _, _ in ways:
                now = sends if part == 2 else both(sends, jnp.logical_not(crosses))
                pl.when(now)(z_copy(up, which, part + 1).start)
    for up, sends, crosses, _, _ in ways:
        pl.when(both(sends, jnp.logical_not(crosses)))(z_copy(up, 1, rest).start)

    for copy in local_copies:
        copy.start()

    for hop in range(1, tm_count):
        for which in range(2):
            text_hop(which, hop)

    blank = jnp.zeros((rows, cols, feat), values.dtype)
    short = jnp.zeros((rows, cols, HD), values.dtype)

    def clear_group(slot):
        for frame in (0, 1, frames, frames + 1):
            values[slot, frame] = blank

        @pl.loop(2, frames)
        def _(frame):
            for head in range(1, heads, 2):
                values[slot, frame, :, :, head * HD : (head + 1) * HD] = short

    def clear_frame(frame):
        for slot in range(3):
            values[slot, frame] = blank

    pl.when(relays_down)(lambda: clear_group(0))
    pl.when(relays_up)(lambda: clear_group(2))
    pl.when(jnp.logical_not(has_before))(lambda: clear_frame(0))
    pl.when(jnp.logical_not(has_after))(lambda: clear_frame(frames + 1))

    for copy in first_copies:
        copy.wait()
    frame_total, tile_count, row_total = table.shape
    span = 3 * tokens
    row_at = lax.broadcasted_iota(jnp.int32, (row_total, span), 0)
    lane_at = lax.broadcasted_iota(jnp.int32, (row_total, span), 1)
    row_hit = row_at == s * rows - rows + lane_at // cols
    tile_at = (lane_at // TILE) % tile_count
    high_part = jnp.zeros((frame_total, span), jnp.float32)
    low_part = jnp.zeros((frame_total, span), jnp.float32)
    for tile in range(tile_count):
        pick = jnp.logical_and(row_hit, tile_at == tile).astype(jnp.float32).astype(jnp.bfloat16)
        column = table[:, tile, :]
        for_high = (column // 128).astype(jnp.float32).astype(jnp.bfloat16)
        for_low = (column % 128).astype(jnp.float32).astype(jnp.bfloat16)
        high_part += jnp.dot(for_high, pick, preferred_element_type=jnp.float32)
        low_part += jnp.dot(for_low, pick, preferred_element_type=jnp.float32)
    near_frames = frames + 2
    frame_at = lax.broadcasted_iota(jnp.int32, (2 * frames, frame_total), 1)
    wanted = lax.broadcasted_iota(jnp.int32, (2 * frames, frame_total), 0) + t * frames - 1
    pick = (frame_at == wanted).astype(jnp.float32).astype(jnp.bfloat16)
    near_high = jnp.dot(pick, high_part.astype(jnp.bfloat16), preferred_element_type=jnp.float32)
    near_low = jnp.dot(pick, low_part.astype(jnp.bfloat16), preferred_element_type=jnp.float32)
    near_ids = near_high * 128.0 + near_low
    for frame in range(near_frames):
        ids[frame] = jnp.broadcast_to(near_ids[frame : frame + 1, :], (8, span))

    @pl.loop(0, frames)
    def _(frame):
        row = ids[frame + 1, 0:1, tokens : 2 * tokens]
        query_ids[frame] = jnp.transpose(jnp.broadcast_to(row, (tokens, tokens)))

    def pass_on(part, which):
        for up, _, _, relays, _ in ways:

            @pl.when(relays)
            def _(up=up):
                z_copy(up, which, part, 1).wait_recv()
                z_copy(up, which, part, 2).start()

    for part in range(2):
        forward = part == 1
        for which in range(2):
            for up, _, _, _, receives in ways:
                slot = 0 if up else 2
                pl.when(receives)(z_copy(up, which, part).wait_recv)
                pl.when(passes_corner(forward, slot))(t_copy(forward, which, slot).start)

    for copy in local_copies:
        copy.wait()

    def wait_halo(which):
        for slot, there in ((1, None), (0, has_low), (2, has_high)):
            for forward, comes in ((True, has_before), (False, has_after)):
                arrives = comes if there is None else both(comes, there)
                pl.when(arrives)(t_copy(forward, which, slot).wait_recv)

    scale = math.log2(math.e) / math.sqrt(HD)
    text_allowed = lax.broadcasted_iota(jnp.int32, (tokens, text_total), 1) < count[0]

    @pl.loop(0, heads)
    def _(head):
        lanes = pl.ds(pl.multiple_of(head * HD, HD), HD)

        @pl.when(head < heads // 2)
        def _():
            for which in range(2):
                pass_on(2 * head + 2, which)

        for up, _, _, _, receives in ways:
            pl.when(receives)(z_copy(up, 0, head + 2).wait_recv)

        for now in range(0, heads - 2, 2):
            for which in range(2):
                for up, _, crosses, _, _ in ways:
                    pl.when(both(crosses, head == now))(z_copy(up, which, now + 5).start)
        for up, _, crosses, _, _ in ways:
            pl.when(both(crosses, head == heads - 4))(z_copy(up, 1, rest).start)

        @pl.when(head == 0)
        def _():
            wait_halo(0)

        @pl.loop(0, frames, unroll=True)
        def _(frame):
            query = queries[frame, :, :, lanes].reshape(tokens, HD)
            own = query_ids[frame]
            near = pl.ds(frame, 3)
            scores = []
            for slot in range(3):
                key = keys[slot, near, :, :, lanes].reshape(3 * tokens, HD)
                raw = lax.dot_general(query, key, NT, preferred_element_type=jnp.float32)
                for j in range(3):
                    there = ids[frame + j, 0:1, slot * tokens : (slot + 1) * tokens]
                    piece = raw[:, j * tokens : (j + 1) * tokens]
                    scores.append(jnp.where(own == there, piece, -jnp.inf))
            raw = lax.dot_general(
                query, text_keys[:, lanes], NT, preferred_element_type=jnp.float32
            )
            scores.append(jnp.where(text_allowed, raw, -jnp.inf))
            highest = jnp.max(functools.reduce(jnp.maximum, scores), axis=1, keepdims=True)
            weights = [jnp.exp2((score - highest) * scale) for score in scores]
            denominator = jnp.sum(functools.reduce(jnp.add, weights), axis=1, keepdims=True)
            denominators[frame] = jnp.broadcast_to(denominator, (tokens, HD))
            for j, weight in enumerate(weights):
                weights_ref[frame, :, j * tokens : j * tokens + weight.shape[1]] = weight.astype(
                    jnp.bfloat16
                )

        @pl.when(head == 0)
        def _():
            wait_halo(1)

        for up, _, _, _, receives in ways:
            pl.when(both(receives, head < heads - 1))(z_copy(up, 1, head + 2).wait_recv)
            pl.when(both(receives, head == heads - 1))(z_copy(up, 1, last).wait_recv)

        def attend(frame):
            near = pl.ds(frame, 3)
            total = jnp.dot(
                weights_ref[frame, :, 9 * tokens :],
                text_values[:, lanes],
                preferred_element_type=jnp.float32,
            )
            for slot in range(3):
                value = values[slot, near, :, :, lanes].reshape(3 * tokens, HD)
                weight = weights_ref[frame, :, 3 * slot * tokens : 3 * (slot + 1) * tokens]
                total += jnp.dot(weight, value, preferred_element_type=jnp.float32)
            attended = (total / denominators[frame]).astype(jnp.bfloat16)
            out_ref[frame, :, :, lanes] = attended.reshape(rows, cols, HD)

        pl.loop(0, frames - 3, unroll=True)(attend)
        for up, _, _, _, receives in ways:
            pl.when(both(receives, head == heads - 1))(z_copy(up, 1, rest).wait_recv)
        pl.loop(frames - 3, frames, unroll=True)(attend)

    for part in range(heads + 2):
        for which in range(2):
            for up, sends, _, relays, _ in ways:
                out = jnp.logical_or(sends, relays) if relayed(part) else sends
                pl.when(out)(z_copy(up, which, part).wait_send)
    for up, sends, _, _, _ in ways:
        pl.when(sends)(z_copy(up, 1, rest).wait_send)
    for which in range(2):
        for forward in (True, False):
            for slot in range(3):
                pl.when(passes_corner(forward, slot))(t_copy(forward, which, slot).wait_send)
    for hop in range(tm_count - 1):
        for forward, _, goes in text_ways(hop):
            for which in range(2):
                pl.when(goes)(text_copy(forward, which, hop).wait_send)


def per_device(
    tm_count,
    space_count,
    queries,
    key_rows,
    value_rows,
    text_keys,
    text_values,
    text_count,
    window_table,
):
    frames, rows, cols, feat = queries.shape
    heads = feat // HD
    tokens = rows * cols
    text_total = text_keys.shape[0] * tm_count
    table = jnp.transpose(window_table, (0, 2, 1))
    block = (3, frames + 2, rows, cols, feat)
    anywhere = pl.BlockSpec(memory_space=pl.ANY)
    key_total = 9 * tokens + text_total
    flops = 4 * frames * tokens * key_total * feat
    return pl.pallas_call(
        functools.partial(kernel, tm_count, space_count),
        out_shape=pltpu.VMEM(queries.shape, queries.dtype),
        in_specs=[anywhere] * 7,
        out_specs=pl.BlockSpec(memory_space=pltpu.VMEM),
        scratch_shapes=[
            pltpu.VMEM(queries.shape, queries.dtype),
            pltpu.VMEM(block, key_rows.dtype),
            pltpu.VMEM(block, value_rows.dtype),
            pltpu.VMEM((text_total, feat), text_keys.dtype),
            pltpu.VMEM((text_total, feat), text_values.dtype),
            pltpu.SMEM(text_count.shape, text_count.dtype),
            pltpu.VMEM(table.shape, table.dtype),
            pltpu.VMEM((frames + 2, 8, 3 * tokens), jnp.float32),
            pltpu.VMEM((frames, tokens, tokens), jnp.float32),
            pltpu.VMEM((frames, tokens, key_total), jnp.bfloat16),
            pltpu.VMEM((frames, tokens, HD), jnp.float32),
            pltpu.SemaphoreType.DMA((2, 2, heads + 3)),
            pltpu.SemaphoreType.DMA((2, 2, heads + 3)),
            pltpu.SemaphoreType.DMA((2, 2, 3)),
            pltpu.SemaphoreType.DMA((2, 2, 3)),
            pltpu.SemaphoreType.DMA((2, 2, tm_count)),
            pltpu.SemaphoreType.DMA((2, 2, tm_count)),
            pltpu.SemaphoreType.DMA((7,)),
        ],
        compiler_params=pltpu.CompilerParams(
            collective_id=0, has_side_effects=True, vmem_limit_bytes=56 * 2**20
        ),
        cost_estimate=pl.CostEstimate(
            flops=flops, bytes_accessed=4 * queries.size * 2, transcendentals=0
        ),
    )(text_count, table, queries, key_rows, value_rows, text_keys, text_values)


def solution(mesh):
    in_specs = (
        P("tm", "space", None, "head"),
        P("tm", "space", None, "head"),
        P("tm", "space", None, "head"),
        P("tm", "head"),
        P("tm", "head"),
        P(),
        P(),
    )
    out_specs = P("tm", "space", None, "head")
    return jax.shard_map(
        functools.partial(per_device, mesh.shape["tm"], mesh.shape["space"]),
        mesh=mesh,
        in_specs=in_specs,
        out_specs=out_specs,
        check_vma=False,
    )
```

```python
import functools
import math

import jax
import jax.numpy as jnp
from jax import lax
from jax.experimental import pallas as pl
from jax.experimental.pallas import tpu as pltpu
from jax.sharding import PartitionSpec as P

TILE = 8
HD = 128
MESH = pl.DeviceIdType.MESH
NT = (((1,), (1,)), ((), ()))


def kernel(
    tm_count,
    space_count,
    count_ref,
    table_ref,
    q_ref,
    k_ref,
    v_ref,
    text_k_ref,
    text_v_ref,
    out_ref,
    queries,
    keys,
    values,
    text_keys,
    text_values,
    count,
    table,
    ids,
    query_ids,
    weights_ref,
    denominators,
    z_send,
    z_recv,
    t_send,
    t_recv,
    text_send,
    text_recv,
    local_sem,
    ready,
):
    frames, rows, cols, feat = q_ref.shape
    heads = feat // HD
    tokens = rows * cols
    text_rows = text_k_ref.shape[0]
    text_total = text_keys.shape[0]
    t = lax.axis_index("tm")
    s = lax.axis_index("space")
    has_low, has_high = s > 0, s < space_count - 1
    has_before, has_after = t > 0, t < tm_count - 1
    low, high = lax.rem(s + space_count - 1, space_count), lax.rem(s + 1, space_count)
    before, after = lax.rem(t + tm_count - 1, tm_count), lax.rem(t + 1, tm_count)
    half = space_count // 2
    crosses_up, crosses_down = s == half - 1, s == half
    relays_up, relays_down = s == space_count - 1, s == 0
    sources = ((k_ref, keys), (v_ref, values))

    def both(*conditions):
        return functools.reduce(jnp.logical_and, conditions)

    last, rest = heads + 1, heads + 2

    def place_of(which, part):
        if isinstance(part, int) and part < 2:
            frame = 0 if part == 0 else frames - 1
            return (pl.ds(frame, 1),), (pl.ds(frame + 1, 1),)
        start, size, head = 1, frames - 2, part - 2
        if isinstance(part, int) and which == 1:
            if part == last:
                size = frames - 3
            elif part == rest:
                start, size, head = frames - 2, 1, heads - 1
        lanes = pl.ds(pl.multiple_of(head * HD, HD), HD)
        inner = (slice(None), slice(None), lanes)
        return (pl.ds(start, size), *inner), (pl.ds(start + 1, size), *inner)

    def z_copy(up, which, part, kind=0):
        source, target = sources[which]
        slot = 0 if up else 2
        side = slot // 2
        here, there = place_of(which, part)
        if kind == 0:
            peer = high if up else low
        elif kind == 1:
            peer = space_count - 1 if up else 0
        else:
            peer = half if up else half - 1
        src = target.at[(2 - slot, *there)] if kind == 2 else source.at[here]
        dst = target.at[(2 - slot if kind == 1 else slot, *there)]
        return pltpu.make_async_remote_copy(
            src_ref=src,
            dst_ref=dst,
            send_sem=z_send.at[side, which, part],
            recv_sem=z_recv.at[1 - side if kind == 1 else side, which, part],
            device_id={"space": peer},
            device_id_type=MESH,
        )

    def t_copy(forward, which, slot):
        source, target = sources[which]
        peer = after if forward else before
        frame = frames - 1 if forward else 0
        place = 0 if forward else frames + 1
        if slot == 1:
            src = source.at[pl.ds(frame, 1)]
        else:
            src = target.at[slot, pl.ds(frame + 1, 1)]
        side = 0 if forward else 1
        return pltpu.make_async_remote_copy(
            src_ref=src,
            dst_ref=target.at[slot, pl.ds(place, 1)],
            send_sem=t_send.at[side, which, slot],
            recv_sem=t_recv.at[side, which, slot],
            device_id={"tm": peer},
            device_id_type=MESH,
        )

    def passes_corner(forward, slot):
        goes = has_after if forward else has_before
        return goes if slot == 1 else both(goes, has_low if slot == 0 else has_high)

    own_rows = pl.ds(pl.multiple_of(t * text_rows, text_rows), text_rows)

    def text_copy(forward, which, hop):
        src, target = ((text_k_ref, text_keys), (text_v_ref, text_values))[which]
        slab = lax.rem(t + (tm_count - hop if forward else hop), tm_count)
        place = pl.ds(pl.multiple_of(slab * text_rows, text_rows), text_rows)
        side = 0 if forward else 1
        return pltpu.make_async_remote_copy(
            src_ref=src if hop == 0 else target.at[place],
            dst_ref=target.at[place],
            send_sem=text_send.at[side, which, hop],
            recv_sem=text_recv.at[side, which, hop],
            device_id={"tm": after if forward else before},
            device_id_type=MESH,
        )

    def text_ways(hop):
        return (
            (True, t >= hop, both(t >= hop, has_after)),
            (False, t < tm_count - hop, both(t < tm_count - hop, has_before)),
        )

    def text_hop(which, hop):
        for forward, comes, goes in text_ways(hop):
            if hop > 0:
                pl.when(comes)(text_copy(forward, which, hop - 1).wait_recv)
            if hop < tm_count - 1:
                pl.when(goes)(text_copy(forward, which, hop).start)

    first_copies = [
        pltpu.make_async_copy(count_ref, count, local_sem.at[5]),
        pltpu.make_async_copy(table_ref, table, local_sem.at[6]),
    ]
    local_copies = [
        pltpu.make_async_copy(q_ref, queries, local_sem.at[0]),
        pltpu.make_async_copy(k_ref, keys.at[1, pl.ds(1, frames)], local_sem.at[1]),
        pltpu.make_async_copy(v_ref, values.at[1, pl.ds(1, frames)], local_sem.at[2]),
        pltpu.make_async_copy(text_k_ref, text_keys.at[own_rows], local_sem.at[3]),
        pltpu.make_async_copy(text_v_ref, text_values.at[own_rows], local_sem.at[4]),
    ]

    barrier = pltpu.get_barrier_semaphore()

    for copy in first_copies:
        copy.start()

    def greet(where):
        pl.semaphore_signal(barrier, inc=1, device_id=where, device_id_type=MESH)

    next_chip = both(lax.rem(t, 2) == 1, has_after)
    previous_chip = both(lax.rem(t, 2) == 0, has_before)
    hears_low = both(has_low, jnp.logical_not(crosses_down))
    hears_after = both(has_after, jnp.logical_not(next_chip))
    pl.when(has_low)(lambda: greet({"space": low}))
    pl.when(both(has_high, jnp.logical_not(crosses_up)))(lambda: greet({"space": high}))
    pl.when(both(has_before, jnp.logical_not(previous_chip)))(lambda: greet({"tm": before}))
    pl.when(has_after)(lambda: greet({"tm": after}))

    @pl.when(s == 0)
    def _():
        greet({"space": half - 1})
        greet({"space": half})

    pl.when(crosses_down)(lambda: greet({"space": space_count - 1}))
    pl.when(s == space_count - 1)(lambda: greet({"space": half - 1}))

    def number(*conditions):
        return functools.reduce(jnp.add, [c.astype(jnp.int32) for c in conditions])

    pl.semaphore_wait(
        barrier,
        number(hears_low, has_high, has_before, hears_after)
        + number(crosses_up, crosses_up, crosses_down, s == space_count - 1),
    )

    @pl.when(crosses_up)
    def _():
        for where in (0, half):
            pl.semaphore_signal(
                ready.at[0], inc=1, device_id={"space": where}, device_id_type=MESH
            )

    @pl.when(previous_chip)
    def _():
        pl.semaphore_signal(ready.at[1], inc=1, device_id={"tm": before}, device_id_type=MESH)

    ways = (
        (True, has_high, crosses_up, relays_up, has_low),
        (False, has_low, crosses_down, relays_down, has_high),
    )

    def relayed(part):
        return part % 2 == 0 and part >= 2

    for which in range(2):
        pl.when(hears_after)(text_copy(True, which, 0).start)
        pl.when(has_before)(text_copy(False, which, 0).start)
    for part in range(2):
        for which in range(2):
            pl.when(has_high)(z_copy(True, which, part).start)
            pl.when(hears_low)(z_copy(False, which, part).start)

    @pl.when(jnp.logical_or(crosses_down, s == 0))
    def _():
        pl.semaphore_wait(ready.at[0], 1)

    @pl.when(next_chip)
    def _():
        pl.semaphore_wait(ready.at[1], 1)

    for which in range(2):
        pl.when(next_chip)(text_copy(True, which, 0).start)
    is_outer = jnp.logical_or(s == 0, s == space_count - 1)

    def text_hops():
        for hop in range(1, tm_count):
            for which in range(2):
                text_hop(which, hop)

    pl.when(jnp.logical_not(is_outer))(text_hops)
    for which in range(2):
        pl.when(has_after)(t_copy(True, which, 1).start)
        pl.when(has_before)(t_copy(False, which, 1).start)
    for part in range(2):
        for which in range(2):
            pl.when(crosses_down)(z_copy(False, which, part).start)

    for part in range(2, heads + 2, 2):
        for which in range(2):
            for up, sends, crosses, _, _ in ways:
                straight = both(sends, jnp.logical_not(crosses))
                pl.when(straight)(z_copy(up, which, part).start)
                pl.when(crosses)(z_copy(up, which, part, 1).start)
        for which in range(2):
            for up, sends, crosses, _, _ in ways:
                now = both(sends, jnp.logical_not(crosses))
                pl.when(now)(z_copy(up, which, part + 1).start)
    for up, sends, crosses, _, _ in ways:
        pl.when(both(sends, jnp.logical_not(crosses)))(z_copy(up, 1, rest).start)

    for copy in local_copies:
        copy.start()

    pl.when(is_outer)(text_hops)

    blank = jnp.zeros((rows, cols, feat), values.dtype)
    short = jnp.zeros((rows, cols, HD), values.dtype)

    def clear_group(slot):
        for frame in (0, 1, frames, frames + 1):
            values[slot, frame] = blank

        @pl.loop(2, frames)
        def _(frame):
            for head in range(1, heads, 2):
                values[slot, frame, :, :, head * HD : (head + 1) * HD] = short

    def clear_frame(frame):
        for slot in range(3):
            values[slot, frame] = blank

    pl.when(relays_down)(lambda: clear_group(0))
    pl.when(relays_up)(lambda: clear_group(2))
    pl.when(jnp.logical_not(has_before))(lambda: clear_frame(0))
    pl.when(jnp.logical_not(has_after))(lambda: clear_frame(frames + 1))

    for copy in first_copies:
        copy.wait()
    frame_total, tile_count, row_total = table.shape
    span = 3 * tokens
    row_at = lax.broadcasted_iota(jnp.int32, (row_total, span), 0)
    lane_at = lax.broadcasted_iota(jnp.int32, (row_total, span), 1)
    row_hit = row_at == s * rows - rows + lane_at // cols
    tile_at = (lane_at // TILE) % tile_count
    high_part = jnp.zeros((frame_total, span), jnp.float32)
    low_part = jnp.zeros((frame_total, span), jnp.float32)
    for tile in range(tile_count):
        pick = jnp.logical_and(row_hit, tile_at == tile).astype(jnp.float32).astype(jnp.bfloat16)
        column = table[:, tile, :]
        for_high = (column // 128).astype(jnp.float32).astype(jnp.bfloat16)
        for_low = (column % 128).astype(jnp.float32).astype(jnp.bfloat16)
        high_part += jnp.dot(for_high, pick, preferred_element_type=jnp.float32)
        low_part += jnp.dot(for_low, pick, preferred_element_type=jnp.float32)
    near_frames = frames + 2
    frame_at = lax.broadcasted_iota(jnp.int32, (2 * frames, frame_total), 1)
    wanted = lax.broadcasted_iota(jnp.int32, (2 * frames, frame_total), 0) + t * frames - 1
    pick = (frame_at == wanted).astype(jnp.float32).astype(jnp.bfloat16)
    near_high = jnp.dot(pick, high_part.astype(jnp.bfloat16), preferred_element_type=jnp.float32)
    near_low = jnp.dot(pick, low_part.astype(jnp.bfloat16), preferred_element_type=jnp.float32)
    near_ids = near_high * 128.0 + near_low
    for frame in range(near_frames):
        ids[frame] = jnp.broadcast_to(near_ids[frame : frame + 1, :], (8, span))

    @pl.loop(0, frames)
    def _(frame):
        row = ids[frame + 1, 0:1, tokens : 2 * tokens]
        query_ids[frame] = jnp.transpose(jnp.broadcast_to(row, (tokens, tokens)))

    def pass_on(part, which):
        for up, _, _, relays, _ in ways:

            @pl.when(relays)
            def _(up=up):
                z_copy(up, which, part, 1).wait_recv()
                z_copy(up, which, part, 2).start()

    for part in range(2):
        forward = part == 1
        for which in range(2):
            for up, _, _, _, receives in ways:
                slot = 0 if up else 2
                pl.when(receives)(z_copy(up, which, part).wait_recv)
                pl.when(passes_corner(forward, slot))(t_copy(forward, which, slot).start)

    for copy in local_copies:
        copy.wait()

    def wait_halo(which):
        for slot, there in ((1, None), (0, has_low), (2, has_high)):
            for forward, comes in ((True, has_before), (False, has_after)):
                arrives = comes if there is None else both(comes, there)
                pl.when(arrives)(t_copy(forward, which, slot).wait_recv)

    scale = math.log2(math.e) / math.sqrt(HD)
    text_allowed = lax.broadcasted_iota(jnp.int32, (tokens, text_total), 1) < count[0]

    @pl.loop(0, heads)
    def _(head):
        lanes = pl.ds(pl.multiple_of(head * HD, HD), HD)

        @pl.when(head < heads // 2)
        def _():
            for which in range(2):
                pass_on(2 * head + 2, which)

        for up, _, _, _, receives in ways:
            pl.when(receives)(z_copy(up, 0, head + 2).wait_recv)

        for now, then in [(0, 3), (1, 5), (2, 7)]:
            for which in range(2):
                for up, _, crosses, _, _ in ways:
                    pl.when(both(crosses, head == now))(z_copy(up, which, then).start)
        for up, _, crosses, _, _ in ways:
            pl.when(both(crosses, head == 2))(z_copy(up, 1, rest).start)

        @pl.when(head == 0)
        def _():
            wait_halo(0)

        @pl.loop(0, frames, unroll=True)
        def _(frame):
            query = queries[frame, :, :, lanes].reshape(tokens, HD)
            own = query_ids[frame]
            near = pl.ds(frame, 3)
            scores = []
            for slot in range(3):
                key = keys[slot, near, :, :, lanes].reshape(3 * tokens, HD)
                raw = lax.dot_general(query, key, NT, preferred_element_type=jnp.float32)
                for j in range(3):
                    there = ids[frame + j, 0:1, slot * tokens : (slot + 1) * tokens]
                    piece = raw[:, j * tokens : (j + 1) * tokens]
                    scores.append(jnp.where(own == there, piece, -jnp.inf))
            raw = lax.dot_general(
                query, text_keys[:, lanes], NT, preferred_element_type=jnp.float32
            )
            scores.append(jnp.where(text_allowed, raw, -jnp.inf))
            highest = jnp.max(functools.reduce(jnp.maximum, scores), axis=1, keepdims=True)
            weights = [jnp.exp2((score - highest) * scale) for score in scores]
            denominator = jnp.sum(functools.reduce(jnp.add, weights), axis=1, keepdims=True)
            denominators[frame] = jnp.broadcast_to(denominator, (tokens, HD))
            for j, weight in enumerate(weights):
                weights_ref[frame, :, j * tokens : j * tokens + weight.shape[1]] = weight.astype(
                    jnp.bfloat16
                )

        @pl.when(head == 0)
        def _():
            wait_halo(1)

        for up, _, _, _, receives in ways:
            pl.when(both(receives, head < heads - 1))(z_copy(up, 1, head + 2).wait_recv)
            pl.when(both(receives, head == heads - 1))(z_copy(up, 1, last).wait_recv)

        def attend(frame):
            near = pl.ds(frame, 3)
            total = jnp.dot(
                weights_ref[frame, :, 9 * tokens :],
                text_values[:, lanes],
                preferred_element_type=jnp.float32,
            )
            for slot in range(3):
                value = values[slot, near, :, :, lanes].reshape(3 * tokens, HD)
                weight = weights_ref[frame, :, 3 * slot * tokens : 3 * (slot + 1) * tokens]
                total += jnp.dot(weight, value, preferred_element_type=jnp.float32)
            attended = (total / denominators[frame]).astype(jnp.bfloat16)
            out_ref[frame, :, :, lanes] = attended.reshape(rows, cols, HD)

        pl.loop(0, frames - 3, unroll=True)(attend)
        for up, _, _, _, receives in ways:
            pl.when(both(receives, head == heads - 1))(z_copy(up, 1, rest).wait_recv)
        pl.loop(frames - 3, frames, unroll=True)(attend)

    for part in range(heads + 2):
        for which in range(2):
            for up, sends, _, relays, _ in ways:
                out = jnp.logical_or(sends, relays) if relayed(part) else sends
                pl.when(out)(z_copy(up, which, part).wait_send)
    for up, sends, _, _, _ in ways:
        pl.when(sends)(z_copy(up, 1, rest).wait_send)
    for which in range(2):
        for forward in (True, False):
            for slot in range(3):
                pl.when(passes_corner(forward, slot))(t_copy(forward, which, slot).wait_send)
    for hop in range(tm_count - 1):
        for forward, _, goes in text_ways(hop):
            for which in range(2):
                pl.when(goes)(text_copy(forward, which, hop).wait_send)


def per_device(
    tm_count,
    space_count,
    queries,
    key_rows,
    value_rows,
    text_keys,
    text_values,
    text_count,
    window_table,
):
    frames, rows, cols, feat = queries.shape
    heads = feat // HD
    tokens = rows * cols
    text_total = text_keys.shape[0] * tm_count
    table = jnp.transpose(window_table, (0, 2, 1))
    block = (3, frames + 2, rows, cols, feat)
    anywhere = pl.BlockSpec(memory_space=pl.ANY)
    key_total = 9 * tokens + text_total
    flops = 4 * frames * tokens * key_total * feat
    return pl.pallas_call(
        functools.partial(kernel, tm_count, space_count),
        out_shape=pltpu.VMEM(queries.shape, queries.dtype),
        in_specs=[anywhere] * 7,
        out_specs=pl.BlockSpec(memory_space=pltpu.VMEM),
        scratch_shapes=[
            pltpu.VMEM(queries.shape, queries.dtype),
            pltpu.VMEM(block, key_rows.dtype),
            pltpu.VMEM(block, value_rows.dtype),
            pltpu.VMEM((text_total, feat), text_keys.dtype),
            pltpu.VMEM((text_total, feat), text_values.dtype),
            pltpu.SMEM(text_count.shape, text_count.dtype),
            pltpu.VMEM(table.shape, table.dtype),
            pltpu.VMEM((frames + 2, 8, 3 * tokens), jnp.float32),
            pltpu.VMEM((frames, tokens, tokens), jnp.float32),
            pltpu.VMEM((frames, tokens, key_total), jnp.bfloat16),
            pltpu.VMEM((frames, tokens, HD), jnp.float32),
            pltpu.SemaphoreType.DMA((2, 2, heads + 3)),
            pltpu.SemaphoreType.DMA((2, 2, heads + 3)),
            pltpu.SemaphoreType.DMA((2, 2, 3)),
            pltpu.SemaphoreType.DMA((2, 2, 3)),
            pltpu.SemaphoreType.DMA((2, 2, tm_count)),
            pltpu.SemaphoreType.DMA((2, 2, tm_count)),
            pltpu.SemaphoreType.DMA((7,)),
            pltpu.SemaphoreType.REGULAR((2,)),
        ],
        compiler_params=pltpu.CompilerParams(
            collective_id=0, has_side_effects=True, vmem_limit_bytes=56 * 2**20
        ),
        cost_estimate=pl.CostEstimate(
            flops=flops, bytes_accessed=4 * queries.size * 2, transcendentals=0
        ),
    )(text_count, table, queries, key_rows, value_rows, text_keys, text_values)


def solution(mesh):
    in_specs = (
        P("tm", "space", None, "head"),
        P("tm", "space", None, "head"),
        P("tm", "space", None, "head"),
        P("tm", "head"),
        P("tm", "head"),
        P(),
        P(),
    )
    out_specs = P("tm", "space", None, "head")
    return jax.shard_map(
        functools.partial(per_device, mesh.shape["tm"], mesh.shape["space"]),
        mesh=mesh,
        in_specs=in_specs,
        out_specs=out_specs,
        check_vma=False,
    )
```

```python
import functools
import math

import jax
import jax.numpy as jnp
from jax import lax
from jax.experimental import pallas as pl
from jax.experimental.pallas import tpu as pltpu
from jax.sharding import PartitionSpec as P

TILE = 8
HD = 128
MESH = pl.DeviceIdType.MESH
NT = (((1,), (1,)), ((), ()))


def kernel(
    tm_count,
    space_count,
    count_ref,
    table_ref,
    q_ref,
    k_ref,
    v_ref,
    text_k_ref,
    text_v_ref,
    out_ref,
    queries,
    keys,
    values,
    text_keys,
    text_values,
    count,
    table,
    ids,
    query_ids,
    weights_ref,
    denominators,
    z_send,
    z_recv,
    t_send,
    t_recv,
    text_send,
    text_recv,
    local_sem,
    ready,
):
    frames, rows, cols, feat = q_ref.shape
    heads = feat // HD
    tokens = rows * cols
    text_rows = text_k_ref.shape[0]
    text_total = text_keys.shape[0]
    t = lax.axis_index("tm")
    s = lax.axis_index("space")
    has_low, has_high = s > 0, s < space_count - 1
    has_before, has_after = t > 0, t < tm_count - 1
    low, high = lax.rem(s + space_count - 1, space_count), lax.rem(s + 1, space_count)
    before, after = lax.rem(t + tm_count - 1, tm_count), lax.rem(t + 1, tm_count)
    half = space_count // 2
    crosses_up, crosses_down = s == half - 1, s == half
    relays_up, relays_down = s == space_count - 1, s == 0
    sources = ((k_ref, keys), (v_ref, values))

    def both(*conditions):
        return functools.reduce(jnp.logical_and, conditions)

    last, rest = heads + 1, heads + 2

    def place_of(which, part):
        if isinstance(part, int) and part < 2:
            frame = 0 if part == 0 else frames - 1
            return (pl.ds(frame, 1),), (pl.ds(frame + 1, 1),)
        start, size, head = 1, frames - 2, part - 2
        if isinstance(part, int) and which == 1:
            if part == last:
                size = frames - 3
            elif part == rest:
                start, size, head = frames - 2, 1, heads - 1
        lanes = pl.ds(pl.multiple_of(head * HD, HD), HD)
        inner = (slice(None), slice(None), lanes)
        return (pl.ds(start, size), *inner), (pl.ds(start + 1, size), *inner)

    def z_copy(up, which, part, kind=0):
        source, target = sources[which]
        slot = 0 if up else 2
        side = slot // 2
        here, there = place_of(which, part)
        if kind == 0:
            peer = high if up else low
        elif kind == 1:
            peer = space_count - 1 if up else 0
        else:
            peer = half if up else half - 1
        src = target.at[(2 - slot, *there)] if kind == 2 else source.at[here]
        dst = target.at[(2 - slot if kind == 1 else slot, *there)]
        return pltpu.make_async_remote_copy(
            src_ref=src,
            dst_ref=dst,
            send_sem=z_send.at[side, which, part],
            recv_sem=z_recv.at[1 - side if kind == 1 else side, which, part],
            device_id={"space": peer},
            device_id_type=MESH,
        )

    def t_copy(forward, which, slot):
        source, target = sources[which]
        peer = after if forward else before
        frame = frames - 1 if forward else 0
        place = 0 if forward else frames + 1
        if slot == 1:
            src = source.at[pl.ds(frame, 1)]
        else:
            src = target.at[slot, pl.ds(frame + 1, 1)]
        side = 0 if forward else 1
        return pltpu.make_async_remote_copy(
            src_ref=src,
            dst_ref=target.at[slot, pl.ds(place, 1)],
            send_sem=t_send.at[side, which, slot],
            recv_sem=t_recv.at[side, which, slot],
            device_id={"tm": peer},
            device_id_type=MESH,
        )

    def passes_corner(forward, slot):
        goes = has_after if forward else has_before
        return goes if slot == 1 else both(goes, has_low if slot == 0 else has_high)

    own_rows = pl.ds(pl.multiple_of(t * text_rows, text_rows), text_rows)

    def text_copy(forward, which, hop):
        src, target = ((text_k_ref, text_keys), (text_v_ref, text_values))[which]
        slab = lax.rem(t + (tm_count - hop if forward else hop), tm_count)
        place = pl.ds(pl.multiple_of(slab * text_rows, text_rows), text_rows)
        side = 0 if forward else 1
        return pltpu.make_async_remote_copy(
            src_ref=src if hop == 0 else target.at[place],
            dst_ref=target.at[place],
            send_sem=text_send.at[side, which, hop],
            recv_sem=text_recv.at[side, which, hop],
            device_id={"tm": after if forward else before},
            device_id_type=MESH,
        )

    def text_ways(hop):
        return (
            (True, t >= hop, both(t >= hop, has_after)),
            (False, t < tm_count - hop, both(t < tm_count - hop, has_before)),
        )

    def text_hop(which, hop):
        for forward, comes, goes in text_ways(hop):
            if hop > 0:
                pl.when(comes)(text_copy(forward, which, hop - 1).wait_recv)
            if hop < tm_count - 1:
                pl.when(goes)(text_copy(forward, which, hop).start)

    first_copies = [
        pltpu.make_async_copy(count_ref, count, local_sem.at[5]),
        pltpu.make_async_copy(table_ref, table, local_sem.at[6]),
    ]
    local_copies = [
        pltpu.make_async_copy(q_ref, queries, local_sem.at[0]),
        pltpu.make_async_copy(k_ref, keys.at[1, pl.ds(1, frames)], local_sem.at[1]),
        pltpu.make_async_copy(v_ref, values.at[1, pl.ds(1, frames)], local_sem.at[2]),
        pltpu.make_async_copy(text_k_ref, text_keys.at[own_rows], local_sem.at[3]),
        pltpu.make_async_copy(text_v_ref, text_values.at[own_rows], local_sem.at[4]),
    ]

    barrier = pltpu.get_barrier_semaphore()

    for copy in first_copies:
        copy.start()

    def greet(where):
        pl.semaphore_signal(barrier, inc=1, device_id=where, device_id_type=MESH)

    next_chip = both(lax.rem(t, 2) == 1, has_after)
    previous_chip = both(lax.rem(t, 2) == 0, has_before)
    hears_low = both(has_low, jnp.logical_not(crosses_down))
    hears_after = both(has_after, jnp.logical_not(next_chip))
    pl.when(has_low)(lambda: greet({"space": low}))
    pl.when(both(has_high, jnp.logical_not(crosses_up)))(lambda: greet({"space": high}))
    pl.when(both(has_before, jnp.logical_not(previous_chip)))(lambda: greet({"tm": before}))
    pl.when(has_after)(lambda: greet({"tm": after}))

    @pl.when(s == 0)
    def _():
        greet({"space": half - 1})
        greet({"space": half})

    pl.when(crosses_down)(lambda: greet({"space": space_count - 1}))
    pl.when(s == space_count - 1)(lambda: greet({"space": half - 1}))

    def number(*conditions):
        return functools.reduce(jnp.add, [c.astype(jnp.int32) for c in conditions])

    pl.semaphore_wait(
        barrier,
        number(hears_low, has_high, has_before, hears_after)
        + number(crosses_up, crosses_up, crosses_down, s == space_count - 1),
    )

    @pl.when(crosses_up)
    def _():
        for where in (0, half):
            pl.semaphore_signal(
                ready.at[0], inc=1, device_id={"space": where}, device_id_type=MESH
            )

    @pl.when(previous_chip)
    def _():
        pl.semaphore_signal(ready.at[1], inc=1, device_id={"tm": before}, device_id_type=MESH)

    ways = (
        (True, has_high, crosses_up, relays_up, has_low),
        (False, has_low, crosses_down, relays_down, has_high),
    )

    def relayed(part):
        return part % 2 == 0 and part >= 2

    for which in range(2):
        pl.when(hears_after)(text_copy(True, which, 0).start)
        pl.when(has_before)(text_copy(False, which, 0).start)
    for part in range(2):
        for which in range(2):
            pl.when(has_high)(z_copy(True, which, part).start)
            pl.when(hears_low)(z_copy(False, which, part).start)

    @pl.when(jnp.logical_or(crosses_down, s == 0))
    def _():
        pl.semaphore_wait(ready.at[0], 1)

    @pl.when(next_chip)
    def _():
        pl.semaphore_wait(ready.at[1], 1)

    for which in range(2):
        pl.when(next_chip)(text_copy(True, which, 0).start)
    is_outer = jnp.logical_or(s == 0, s == space_count - 1)

    def text_hops():
        for hop in range(1, tm_count):
            for which in range(2):
                text_hop(which, hop)

    pl.when(jnp.logical_not(is_outer))(text_hops)
    for which in range(2):
        pl.when(has_after)(t_copy(True, which, 1).start)
        pl.when(has_before)(t_copy(False, which, 1).start)
    for part in range(2):
        for which in range(2):
            pl.when(crosses_down)(z_copy(False, which, part).start)

    for part in range(2, heads + 2, 2):
        for which in range(2):
            for up, sends, crosses, _, _ in ways:
                straight = both(sends, jnp.logical_not(crosses))
                pl.when(straight)(z_copy(up, which, part).start)
                pl.when(crosses)(z_copy(up, which, part, 1).start)
        for which in range(2):
            for up, sends, crosses, _, _ in ways:
                now = both(sends, jnp.logical_not(crosses))
                pl.when(now)(z_copy(up, which, part + 1).start)
    for up, sends, crosses, _, _ in ways:
        pl.when(both(sends, jnp.logical_not(crosses)))(z_copy(up, 1, rest).start)

    for copy in local_copies:
        copy.start()

    pl.when(is_outer)(text_hops)

    blank = jnp.zeros((rows, cols, feat), values.dtype)
    short = jnp.zeros((rows, cols, HD), values.dtype)

    def clear_group(slot):
        for frame in (0, 1, frames, frames + 1):
            values[slot, frame] = blank

        @pl.loop(2, frames)
        def _(frame):
            for head in range(1, heads, 2):
                values[slot, frame, :, :, head * HD : (head + 1) * HD] = short

    def clear_frame(frame):
        for slot in range(3):
            values[slot, frame] = blank

    pl.when(relays_down)(lambda: clear_group(0))
    pl.when(relays_up)(lambda: clear_group(2))
    pl.when(jnp.logical_not(has_before))(lambda: clear_frame(0))
    pl.when(jnp.logical_not(has_after))(lambda: clear_frame(frames + 1))

    for copy in first_copies:
        copy.wait()
    frame_total, tile_count, row_total = table.shape
    span = 3 * tokens
    row_at = lax.broadcasted_iota(jnp.int32, (row_total, span), 0)
    lane_at = lax.broadcasted_iota(jnp.int32, (row_total, span), 1)
    row_hit = row_at == s * rows - rows + lane_at // cols
    tile_at = (lane_at // TILE) % tile_count
    high_part = jnp.zeros((frame_total, span), jnp.float32)
    low_part = jnp.zeros((frame_total, span), jnp.float32)
    for tile in range(tile_count):
        pick = jnp.logical_and(row_hit, tile_at == tile).astype(jnp.float32).astype(jnp.bfloat16)
        column = table[:, tile, :]
        for_high = (column // 128).astype(jnp.float32).astype(jnp.bfloat16)
        for_low = (column % 128).astype(jnp.float32).astype(jnp.bfloat16)
        high_part += jnp.dot(for_high, pick, preferred_element_type=jnp.float32)
        low_part += jnp.dot(for_low, pick, preferred_element_type=jnp.float32)
    near_frames = frames + 2
    frame_at = lax.broadcasted_iota(jnp.int32, (2 * frames, frame_total), 1)
    wanted = lax.broadcasted_iota(jnp.int32, (2 * frames, frame_total), 0) + t * frames - 1
    pick = (frame_at == wanted).astype(jnp.float32).astype(jnp.bfloat16)
    near_high = jnp.dot(pick, high_part.astype(jnp.bfloat16), preferred_element_type=jnp.float32)
    near_low = jnp.dot(pick, low_part.astype(jnp.bfloat16), preferred_element_type=jnp.float32)
    near_ids = near_high * 128.0 + near_low
    for frame in range(near_frames):
        ids[frame] = jnp.broadcast_to(near_ids[frame : frame + 1, :], (8, span))

    @pl.loop(0, frames)
    def _(frame):
        row = ids[frame + 1, 0:1, tokens : 2 * tokens]
        query_ids[frame] = jnp.transpose(jnp.broadcast_to(row, (tokens, tokens)))

    def pass_on(part, which):
        for up, _, _, relays, _ in ways:

            @pl.when(relays)
            def _(up=up):
                z_copy(up, which, part, 1).wait_recv()
                z_copy(up, which, part, 2).start()

    for part in range(2):
        forward = part == 1
        for which in range(2):
            for up, _, _, _, receives in ways:
                slot = 0 if up else 2
                pl.when(receives)(z_copy(up, which, part).wait_recv)
                pl.when(passes_corner(forward, slot))(t_copy(forward, which, slot).start)

    for copy in local_copies:
        copy.wait()

    def wait_halo(which):
        for slot, there in ((1, None), (0, has_low), (2, has_high)):
            for forward, comes in ((True, has_before), (False, has_after)):
                arrives = comes if there is None else both(comes, there)
                pl.when(arrives)(t_copy(forward, which, slot).wait_recv)

    scale = math.log2(math.e) / math.sqrt(HD)
    text_allowed = lax.broadcasted_iota(jnp.int32, (tokens, text_total), 1) < count[0]

    def wait_sent():
        for part in range(last):
            for which in range(2):
                for up, sends, _, relays, _ in ways:
                    out = jnp.logical_or(sends, relays) if relayed(part) else sends
                    pl.when(out)(z_copy(up, which, part).wait_send)
        for which in range(2):
            for forward in (True, False):
                for slot in range(3):
                    pl.when(passes_corner(forward, slot))(t_copy(forward, which, slot).wait_send)
        for hop in range(tm_count - 1):
            for forward, _, goes in text_ways(hop):
                for which in range(2):
                    pl.when(goes)(text_copy(forward, which, hop).wait_send)

    @pl.loop(0, heads)
    def _(head):
        lanes = pl.ds(pl.multiple_of(head * HD, HD), HD)

        @pl.when(head < heads // 2)
        def _():
            for which in range(2):
                pass_on(2 * head + 2, which)

        for up, _, _, _, receives in ways:
            pl.when(receives)(z_copy(up, 0, head + 2).wait_recv)

        for now, then in [(0, 3), (1, 5), (2, 7)]:
            for which in range(2):
                for up, _, crosses, _, _ in ways:
                    pl.when(both(crosses, head == now))(z_copy(up, which, then).start)
        for up, _, crosses, _, _ in ways:
            pl.when(both(crosses, head == 2))(z_copy(up, 1, rest).start)

        @pl.when(head == 0)
        def _():
            wait_halo(0)

        @pl.loop(0, frames, unroll=True)
        def _(frame):
            query = queries[frame, :, :, lanes].reshape(tokens, HD)
            own = query_ids[frame]
            near = pl.ds(frame, 3)
            scores = []
            for slot in range(3):
                key = keys[slot, near, :, :, lanes].reshape(3 * tokens, HD)
                raw = lax.dot_general(query, key, NT, preferred_element_type=jnp.float32)
                for j in range(3):
                    there = ids[frame + j, 0:1, slot * tokens : (slot + 1) * tokens]
                    piece = raw[:, j * tokens : (j + 1) * tokens]
                    scores.append(jnp.where(own == there, piece, -jnp.inf))
            raw = lax.dot_general(
                query, text_keys[:, lanes], NT, preferred_element_type=jnp.float32
            )
            scores.append(jnp.where(text_allowed, raw, -jnp.inf))
            highest = jnp.max(functools.reduce(jnp.maximum, scores), axis=1, keepdims=True)
            weights = [jnp.exp2((score - highest) * scale) for score in scores]
            denominator = jnp.sum(functools.reduce(jnp.add, weights), axis=1, keepdims=True)
            denominators[frame] = jnp.broadcast_to(denominator, (tokens, HD))
            for j, weight in enumerate(weights):
                weights_ref[frame, :, j * tokens : j * tokens + weight.shape[1]] = weight.astype(
                    jnp.bfloat16
                )

        @pl.when(head == 0)
        def _():
            wait_halo(1)

        pl.when(head == heads - 1)(wait_sent)
        for up, _, _, _, receives in ways:
            pl.when(both(receives, head < heads - 1))(z_copy(up, 1, head + 2).wait_recv)
            pl.when(both(receives, head == heads - 1))(z_copy(up, 1, last).wait_recv)

        def attend(frame):
            near = pl.ds(frame, 3)
            total = jnp.dot(
                weights_ref[frame, :, 9 * tokens :],
                text_values[:, lanes],
                preferred_element_type=jnp.float32,
            )
            for slot in range(3):
                value = values[slot, near, :, :, lanes].reshape(3 * tokens, HD)
                weight = weights_ref[frame, :, 3 * slot * tokens : 3 * (slot + 1) * tokens]
                total += jnp.dot(weight, value, preferred_element_type=jnp.float32)
            attended = (total / denominators[frame]).astype(jnp.bfloat16)
            out_ref[frame, :, :, lanes] = attended.reshape(rows, cols, HD)

        pl.loop(0, frames - 3, unroll=True)(attend)
        for up, _, _, _, receives in ways:
            pl.when(both(receives, head == heads - 1))(z_copy(up, 1, rest).wait_recv)
        pl.loop(frames - 3, frames, unroll=True)(attend)

    for part in range(last, heads + 2):
        for which in range(2):
            for up, sends, _, relays, _ in ways:
                out = jnp.logical_or(sends, relays) if relayed(part) else sends
                pl.when(out)(z_copy(up, which, part).wait_send)
    for up, sends, _, _, _ in ways:
        pl.when(sends)(z_copy(up, 1, rest).wait_send)

def per_device(
    tm_count,
    space_count,
    queries,
    key_rows,
    value_rows,
    text_keys,
    text_values,
    text_count,
    window_table,
):
    frames, rows, cols, feat = queries.shape
    heads = feat // HD
    tokens = rows * cols
    text_total = text_keys.shape[0] * tm_count
    table = jnp.transpose(window_table, (0, 2, 1))
    block = (3, frames + 2, rows, cols, feat)
    anywhere = pl.BlockSpec(memory_space=pl.ANY)
    key_total = 9 * tokens + text_total
    flops = 4 * frames * tokens * key_total * feat
    return pl.pallas_call(
        functools.partial(kernel, tm_count, space_count),
        out_shape=pltpu.VMEM(queries.shape, queries.dtype),
        in_specs=[anywhere] * 7,
        out_specs=pl.BlockSpec(memory_space=pltpu.VMEM),
        scratch_shapes=[
            pltpu.VMEM(queries.shape, queries.dtype),
            pltpu.VMEM(block, key_rows.dtype),
            pltpu.VMEM(block, value_rows.dtype),
            pltpu.VMEM((text_total, feat), text_keys.dtype),
            pltpu.VMEM((text_total, feat), text_values.dtype),
            pltpu.SMEM(text_count.shape, text_count.dtype),
            pltpu.VMEM(table.shape, table.dtype),
            pltpu.VMEM((frames + 2, 8, 3 * tokens), jnp.float32),
            pltpu.VMEM((frames, tokens, tokens), jnp.float32),
            pltpu.VMEM((frames, tokens, key_total), jnp.bfloat16),
            pltpu.VMEM((frames, tokens, HD), jnp.float32),
            pltpu.SemaphoreType.DMA((2, 2, heads + 3)),
            pltpu.SemaphoreType.DMA((2, 2, heads + 3)),
            pltpu.SemaphoreType.DMA((2, 2, 3)),
            pltpu.SemaphoreType.DMA((2, 2, 3)),
            pltpu.SemaphoreType.DMA((2, 2, tm_count)),
            pltpu.SemaphoreType.DMA((2, 2, tm_count)),
            pltpu.SemaphoreType.DMA((7,)),
            pltpu.SemaphoreType.REGULAR((2,)),
        ],
        compiler_params=pltpu.CompilerParams(
            collective_id=0, has_side_effects=True, vmem_limit_bytes=56 * 2**20
        ),
        cost_estimate=pl.CostEstimate(
            flops=flops, bytes_accessed=4 * queries.size * 2, transcendentals=0
        ),
    )(text_count, table, queries, key_rows, value_rows, text_keys, text_values)


def solution(mesh):
    in_specs = (
        P("tm", "space", None, "head"),
        P("tm", "space", None, "head"),
        P("tm", "space", None, "head"),
        P("tm", "head"),
        P("tm", "head"),
        P(),
        P(),
    )
    out_specs = P("tm", "space", None, "head")
    return jax.shard_map(
        functools.partial(per_device, mesh.shape["tm"], mesh.shape["space"]),
        mesh=mesh,
        in_specs=in_specs,
        out_specs=out_specs,
        check_vma=False,
    )
```
